256 devices in a mesh: band: 2 (over z_hi), domain: 128 (over x, y, z_lo, core).
Axes of the slice: x: 4, y: 4, z: 8 (z_hi: 2, z_lo: 4; z = z_hi * 4 + z_lo), core: 2. Of those that a mesh axis runs over, the one named last changes fastest.
Arguments:
- orbitals: bfloat16 [1024, 128, 2048], P('band', 'domain')
- potential: float32 [128, 2048], P('domain'), may hold values from 0.25 to 6
Outputs:
- rotated: bfloat16 [1024, 128, 2048], P('band', 'domain')
- h_sub: float32 [1024, 1024], replicated
The draws below stay inside these ranges and needn't reach their ends.
All inputs are finite; a program needn't handle non-finite values.
Results may differ from the reference program's by a relative error of at most 0.0058.
Values may be sent and summed in bfloat16 or wider, within the bound.
A program may use at most 128 MiB of HBM per device.

```python
import jax
import jax.numpy as jnp
from jax import lax

ORB = 1024
BX = 4
BY = 4
NZ = 128
PY = 8
BLOCKS = 128
CELLS = 2048
NX = 64
NY = 32


def draw_orbitals(key, part):
    key = jax.random.fold_in(key, 11)
    base_key = jax.random.fold_in(key, 0)
    order_key = jax.random.fold_in(key, 2)
    phase_key = jax.random.fold_in(key, 3)
    shape = (ORB, BLOCKS, CELLS)
    base = jax.random.normal(base_key, shape, jnp.float32)
    order = jax.random.permutation(order_key, BLOCKS).astype(jnp.int32)
    index = lax.broadcasted_iota(jnp.int32, (ORB,), 0)
    slot = index % (2 * BLOCKS)
    kind = slot // BLOCKS
    anchor = order[slot % BLOCKS]
    anchor_x = anchor // PY
    anchor_y = anchor % PY
    block = lax.broadcasted_iota(jnp.int32, (BLOCKS,), 0)
    delta_x = (block[None, :] // PY - anchor_x[:, None]) % (BLOCKS // PY)
    delta_y = (block[None, :] % PY - anchor_y[:, None]) % PY
    home = (delta_x == 0) & (delta_y == 0)
    along_x = (kind[:, None] == 0) & (delta_x == 1) & (delta_y == 0)
    along_y = (kind[:, None] == 1) & (delta_x == 0) & (delta_y == 1)
    heavy = home | along_x | along_y
    envelope = jnp.where(heavy, (2.0 * BLOCKS) ** 0.5, 1.0).astype(jnp.float32)
    depth = (lax.broadcasted_iota(jnp.int32, (CELLS,), 0) % NZ).astype(jnp.float32)
    phase = jax.random.uniform(phase_key, (ORB,), jnp.float32, 0.0, 6.2831853)
    smooth = 1.5 * jnp.cos(6.2831853 * depth[None, :] / NZ + phase[:, None])
    values = envelope[:, :, None] * (base + smooth[:, None, :])
    return (values * (1.0 / (2.125 * 5.0 * BLOCKS * CELLS) ** 0.5)).astype(jnp.bfloat16)


def draw_potential(key, part):
    key = jax.random.fold_in(key, 23)
    shape = (BLOCKS, CELLS)
    place = lax.broadcasted_iota(jnp.float32, shape, 0)
    ramp = 1.0 + 2.0 * place / BLOCKS
    level = jax.random.uniform(key, shape, jnp.float32, 0.5, 1.5)
    return level * ramp


def setup_inputs(seed: int = 0) -> dict:
    arg_keys = jax.random.split(jax.random.key(seed), 3)
    orbitals = draw_orbitals(jax.random.fold_in(arg_keys[2], 71), 0)
    potential = draw_potential(jax.random.fold_in(arg_keys[2], 71), 0)
    return dict(orbitals=orbitals, potential=potential)


def to_grid(array, lead):
    shaped = array.reshape(lead + (NX // BX, PY, BX, BY, NZ))
    count = len(lead)
    order = tuple(range(count)) + (count, count + 2, count + 1, count + 3, count + 4)
    return shaped.transpose(order).reshape(lead + (NX, NY, NZ))

def second_all(field):
    total = -90.0 * field
    for axis in (1, 2, 3):
        for step, weight in ((1, 16.0), (2, -1.0)):
            total = total + weight * (jnp.roll(field, step, axis=axis) + jnp.roll(field, -step, axis=axis))
    return total / 12.0

def apply_block(block, vgrid):
    field = block.astype(jnp.float32)
    lap = second_all(field)
    return (-0.5 * lap + vgrid[None] * field).astype(jnp.bfloat16)

def mirror(matrix):
    return jnp.tril(matrix) + jnp.tril(matrix, -1).T

def reference(orbitals, potential):
    grid = to_grid(orbitals, (ORB,))
    vgrid = to_grid(potential, ())
    blocks = grid.reshape((ORB // 16, 16, NX, NY, NZ))
    hpsi = lax.map(lambda blk: apply_block(blk, vgrid), blocks)
    flat = grid.reshape(ORB, -1)
    hflat = hpsi.reshape(ORB, -1)
    intersection = mirror(jnp.dot(flat.astype(jnp.float32), flat.T.astype(jnp.float32), preferred_element_type=jnp.float32))
    ham_hat = mirror(jnp.dot(hflat.astype(jnp.float32), flat.T.astype(jnp.float32), preferred_element_type=jnp.float32))
    vmean = jnp.sum(potential) / (NX * NY * NZ)
    ham = ham_hat - vmean * intersection
    chol = jnp.linalg.cholesky(intersection)
    linv = lax.linalg.triangular_solve(chol, jnp.eye(ORB, dtype=jnp.float32), left_side=True, lower=True)
    h_sub = jnp.dot(jnp.dot(linv, ham, precision=lax.Precision.HIGHEST), linv.T, precision=lax.Precision.HIGHEST)
    rot = linv.astype(jnp.bfloat16)
    rotated = jnp.dot(rot.astype(jnp.float32), orbitals.reshape(ORB, -1).astype(jnp.float32), preferred_element_type=jnp.float32).astype(jnp.bfloat16)
    return (rotated.reshape(orbitals.shape), h_sub)
```

```python
import functools

import jax
import jax.numpy as jnp
from jax import lax
from jax.experimental import pallas as pl
from jax.experimental.pallas import tpu as pltpu
from jax.sharding import PartitionSpec as P

MESH = pl.DeviceIdType.MESH
HI = lax.Precision.HIGHEST
NN = (((1,), (0,)), ((), ()))
NT = (((1,), (1,)), ((), ()))
TN = (((0,), (0,)), ((), ()))
F32 = jnp.float32
BF16 = jnp.bfloat16
VMEM = pl.BlockSpec(memory_space=pltpu.VMEM)
MIB = 2**20
CELLS = 2048
HALF = 512
TILES_UP = ((0, 0), (0, 1), (1, 1))
TILES_LOW = ((0, 0), (1, 0), (1, 1))
TILES_ALL = ((0, 0), (0, 1), (1, 0), (1, 1))


def fdot(a, b, dims=NN):
    return lax.dot_general(a, b, dims, precision=HI, preferred_element_type=F32)


def bdot(a, b, dims=NN):
    return lax.dot_general(a, b, dims, preferred_element_type=F32)


def call(kernel, outs, args, name, scratch=(), collective=None, limit=48, flops=0):
    params = dict(vmem_limit_bytes=limit * MIB)
    if collective is not None:
        params.update(collective_id=collective, has_side_effects=True)
    return pl.pallas_call(
        kernel,
        out_shape=outs,
        in_specs=[VMEM] * len(args),
        out_specs=jax.tree.map(lambda _: VMEM, outs),
        scratch_shapes=list(scratch),
        compiler_params=pltpu.CompilerParams(**params),
        cost_estimate=pl.CostEstimate(flops=flops, bytes_accessed=8 * MIB, transcendentals=0),
        name=name,
    )(*args)


def own_overlap_kernel(orb, pot, pay):
    for t, (r, c) in enumerate(TILES_UP):
        tile = bdot(orb[256 * r : 256 * r + 256, :], orb[256 * c : 256 * c + 256, :], NT)
        pay[2 * t] = tile[:, :128]
        pay[2 * t + 1] = tile[:, 128:]
    pay[0, 128:136, :] = pot[0:8, :] + pot[8:16, :]


def all_sum_kernel(n_both, n_one, *refs):
    refs = list(refs)
    sizes = [(n, mode) for n, mode in ((n_both, "both"), (n_one, "one")) if n]
    n = len(sizes)
    pays, outs, rest = refs[:n], refs[n : 2 * n], refs[2 * n :]
    bufs = [rest[4 * i : 4 * i + 4] for i in range(n)]
    sems = rest[4 * n :]
    s1, r1, s2, r2, s3, r3, s4, r4, s5, r5 = sems
    band = lax.axis_index("band")
    dom = lax.axis_index("domain")
    x, y = dom // 32, (dom // 8) % 4
    z, core = (dom // 2) % 4, dom % 2
    here = x * 4 + y
    zz = band * 4 + z

    def at(b, xx, yy, zl, cc):
        return (b, ((xx * 4 + yy) * 4 + zl) * 2 + cc)

    partner = at(band, x, y, z, 1 - core)

    def xy_peer(k):
        xx, yy = (x + k // 4) % 4, (y + k % 4) % 4
        return at(band, xx, yy, z, core), xx * 4 + yy

    def xy_source(k):
        return ((x + 4 - k // 4) % 4) * 4 + (y + 4 - k % 4) % 4

    def z_peer(k):
        other = (zz + k) % 8
        return at(other // 4, x, y, other % 4, core)

    barrier = pltpu.get_barrier_semaphore()
    pl.semaphore_signal(barrier, inc=1, device_id=partner, device_id_type=MESH)
    for k in range(1, 16):
        pl.semaphore_signal(barrier, inc=1, device_id=xy_peer(k)[0], device_id_type=MESH)
    for k in range(1, 8):
        pl.semaphore_signal(barrier, inc=1, device_id=z_peer(k), device_id_type=MESH)
    pl.semaphore_wait(barrier, 23)

    def when(mode, body, condition=None):
        if mode == "one":
            pl.when(band == 1 if condition is None else condition)(body)
        else:
            body()

    def remote(src, dst, send, recv, device):
        return pltpu.make_async_remote_copy(
            src_ref=src, dst_ref=dst, send_sem=send, recv_sem=recv, device_id=device, device_id_type=MESH
        )

    mine = pl.ds(pl.multiple_of(core * 128, 128), 128)
    theirs = pl.ds(pl.multiple_of((1 - core) * 128, 128), 128)

    firsts = []
    for i, (_, mode) in enumerate(sizes):
        copy = remote(pays[i].at[:, theirs, :], bufs[i][0], s1.at[i], r1.at[i], partner)
        when(mode, copy.start)
        firsts.append(copy)
    seconds = []
    for i, (_, mode) in enumerate(sizes):
        pay, (half, whole, got, _) = pays[i], bufs[i]

        def second(i=i, pay=pay, half=half, whole=whole, got=got):
            firsts[i].wait()
            whole[...] = pay[:, mine, :] + half[...]
            for k in range(1, 16):
                device, there = xy_peer(k)
                rows = pl.ds(pl.multiple_of(there * 8, 8), 8)
                remote(whole.at[:, rows, :], got.at[k], s2.at[i, k], r2.at[i, k], device).start()

        when(mode, second)
    for i, (_, mode) in enumerate(sizes):
        whole, got, along = bufs[i][1:]

        def third(i=i, whole=whole, got=got, along=along):
            rows = pl.ds(pl.multiple_of(here * 8, 8), 8)
            for k in range(1, 16):
                remote(whole.at[:, rows, :], got.at[k], s2.at[i, k], r2.at[i, k], xy_peer(k)[0]).wait()
            total = whole[:, rows, :]
            for k in range(1, 16):
                total = total + got[k]
            along[zz] = total
            for k in range(1, 8):
                remote(along.at[zz], along.at[zz], s3.at[i, k], r3.at[i, k], z_peer(k)).start()

        when(mode, third)
    place = pl.ds(pl.multiple_of(core * 128 + here * 8, 8), 8)

    def spot(out, mode, rows):
        return out.at[:, :, rows, :] if mode == "both" else out.at[:, rows, :]

    for i, (_, mode) in enumerate(sizes):
        along, out = bufs[i][3], outs[i]
        for k in range(1, 8):
            source = (zz + 8 - k) % 8
            copy = remote(along.at[zz], along.at[source], s3.at[i, k], r3.at[i, k], z_peer(k))
            when(mode, copy.wait_send)
            when(mode, copy.wait_recv, source >= 4)
        upper = along[4] + along[5] + along[6] + along[7]
        if mode == "both":
            out[0, :, place, :] = along[0] + along[1] + along[2] + along[3]
            out[1, :, place, :] = upper
        else:
            out[:, place, :] = upper
        for k in range(1, 16):
            here_spot = spot(out, mode, place)
            remote(here_spot, here_spot, s4.at[i, k], r4.at[i, k], xy_peer(k)[0]).start()
        here_spot = spot(out, mode, place)
        remote(here_spot, here_spot, s5.at[i, 0], r5.at[i, 0], partner).start()
    for i, (_, mode) in enumerate(sizes):
        out = outs[i]
        for k in range(1, 16):
            rows = pl.ds(pl.multiple_of(core * 128 + xy_source(k) * 8, 8), 8)
            there = spot(out, mode, rows)
            remote(there, there, s4.at[i, k], r4.at[i, k], xy_peer(k)[0]).wait_recv()
            remote(there, there, s5.at[i, k], r5.at[i, k], partner).start()
    for i, (_, mode) in enumerate(sizes):
        out = outs[i]
        here_spot = spot(out, mode, place)
        for k in range(1, 16):
            remote(here_spot, here_spot, s4.at[i, k], r4.at[i, k], xy_peer(k)[0]).wait_send()
        for k in range(16):
            remote(here_spot, here_spot, s5.at[i, k], r5.at[i, k], partner).wait()


def all_sum(both, one, collective, name):
    args, outs, scratch = [], [], []
    if both is not None:
        args.append(both)
        outs.append(jax.ShapeDtypeStruct((2,) + both.shape, F32))
    if one is not None:
        args.append(one)
        outs.append(jax.ShapeDtypeStruct(one.shape, F32))
    for array in args:
        n = array.shape[0]
        scratch += [
            pltpu.VMEM((n, 128, 128), F32),
            pltpu.VMEM((n, 128, 128), F32),
            pltpu.VMEM((16, n, 8, 128), F32),
            pltpu.VMEM((8, n, 8, 128), F32),
        ]
    n = len(args)
    dma = pltpu.SemaphoreType.DMA
    scratch += [dma((n,)), dma((n,)), dma((n, 16)), dma((n, 16)), dma((n, 8)), dma((n, 8))]
    scratch += [dma((n, 16)), dma((n, 16)), dma((n, 16)), dma((n, 16))]
    n_both = 0 if both is None else both.shape[0]
    n_one = 0 if one is None else one.shape[0]
    return call(
        functools.partial(all_sum_kernel, n_both, n_one),
        outs,
        args,
        name,
        scratch=scratch,
        collective=collective,
        flops=10**9,
    )


def invert_block(block):
    lane = lax.broadcasted_iota(jnp.int32, (8, 128), 1)
    sub = lax.broadcasted_iota(jnp.int32, (8, 128), 0)
    rows = [block[8 * p : 8 * p + 8] for p in range(16)]
    for p in range(16):
        k = 8 * p
        panel = rows[p]
        d = [[jnp.broadcast_to(panel[i : i + 1, k + j : k + j + 1], (8, 128)) for j in range(i + 1)] for i in range(8)]
        inside = (lane >= k) & (lane < k + 8)
        start = jnp.where(inside, (lane == k + sub).astype(F32), panel)
        acc = [jnp.broadcast_to(start[s : s + 1, :], (8, 128)) for s in range(8)]
        done = []
        for j in range(8):
            r = lax.rsqrt(d[j][j])
            xj = acc[j] * r
            done.append(xj)
            low = [None] * 8
            for i in range(j + 1, 8):
                low[i] = d[i][j] * r
            for i in range(j + 1, 8):
                for m in range(j + 1, i + 1):
                    d[i][m] = d[i][m] - low[i] * low[m]
                acc[i] = acc[i] - low[i] * xj
        x = done[0]
        for s in range(1, 8):
            x = jnp.where(sub == s, done[s], x)
        rows[p] = x
        if p < 15:
            right = jnp.where(lane >= k + 8, x, 0.0)
            update = fdot(right, x, TN)
            for q in range(p + 1, 16):
                rows[q] = jnp.where(inside, 0.0, rows[q]) - update[8 * q : 8 * q + 8]
    whole = jnp.concatenate(rows, axis=0)
    rr = lax.broadcasted_iota(jnp.int32, (128, 128), 0)
    cc = lax.broadcasted_iota(jnp.int32, (128, 128), 1)
    return jnp.where(cc <= rr, whole, 0.0)


def eliminate(c, offset):
    blocks = c.shape[0] // 128
    rr = lax.broadcasted_iota(jnp.int32, (128, 128), 0)
    cc = lax.broadcasted_iota(jnp.int32, (128, 128), 1)

    @pl.loop(0, blocks)
    def _(j):
        rows = pl.ds(pl.multiple_of(j * 128, 128), 128)
        cols = pl.ds(pl.multiple_of(offset + j * 128, 128), 128)
        inverse = invert_block(c[rows, cols])
        c[rows, cols] = (rr == cc).astype(F32)
        c[rows, :] = fdot(inverse, c[rows, :])

        @pl.loop(j + 1, blocks)
        def _(i):
            below = pl.ds(pl.multiple_of(i * 128, 128), 128)
            across = pl.ds(pl.multiple_of(offset + i * 128, 128), 128)
            factor = c[rows, across]
            c[below, cols] = jnp.zeros((128, 128), F32)
            c[below, :] = c[below, :] - fdot(factor, c[rows, :], TN)

    for i in range(blocks):
        for j in range(i + 1, blocks):
            c[128 * i : 128 * i + 128, offset + 128 * j : offset + 128 * j + 128] = jnp.zeros((128, 128), F32)


def spread(c, slabs, tiles, offset):
    for t, (r, col) in enumerate(tiles):
        for h in range(2):
            lo = offset + 256 * col + 128 * h
            c[256 * r : 256 * r + 256, lo : lo + 128] = slabs(2 * t + h)


def first_factor_kernel(s, w):
    w[256:512, 0:256] = jnp.zeros((256, 256), F32)
    spread(w, lambda i: s[0, i], TILES_UP, 0)
    eliminate(w, 0)


def split(a):
    high = a.astype(BF16)
    return high, (a - high.astype(F32)).astype(BF16)


def dot3(a, b, dims=NN):
    return bdot(a[0], b[0], dims) + (bdot(a[0], b[1], dims) + bdot(a[1], b[0], dims))


def last_kernel(s, hown, cross, w0, h_sub, rot_other, rot_own, c, cross_s, wh, wl, mh, ml):
    band = lax.axis_index("band")
    for t, (r, col) in enumerate(TILES_ALL):
        for h in range(2):
            lo = 256 * col + 128 * h
            cross_s[256 * r : 256 * r + 256, lo : lo + 128] = cross[2 * t + h]
    low = fdot(cross_s[...], w0[...], NT)
    c[256:512, 512:768] = jnp.zeros((256, 256), F32)
    spread(c, lambda i: s[1, i], TILES_UP, 512)
    c[:, 512:1024] = c[:, 512:1024] - fdot(low, low, NT)
    c[:, 0:512] = -fdot(low, w0[...])
    eliminate(c, 512)

    @pl.when(band == 0)
    def _():
        rot_own[...] = w0[...].astype(BF16)
        rot_other[...] = jnp.zeros((512, 512), BF16)

    @pl.when(band == 1)
    def _():
        rot_own[...] = c[:, 512:1024].astype(BF16)
        rot_other[...] = c[:, 0:512].astype(BF16)

    for r in range(4):
        source = w0 if r < 2 else c
        base = 256 * (r % 2)
        width = 512 if r < 2 else 1024
        high, lowpart = split(source[base : base + 256, :])
        wh[256 * r : 256 * r + 256, 0:width] = high
        wl[256 * r : 256 * r + 256, 0:width] = lowpart

    rr = lax.broadcasted_iota(jnp.int32, (256, 256), 0)
    cc = lax.broadcasted_iota(jnp.int32, (256, 256), 1)
    weight = jnp.where(cc < rr, 1.0, jnp.where(cc == rr, 0.5, 0.0)).astype(F32)

    def pair(slabs, t):
        return jnp.concatenate([slabs(2 * t), slabs(2 * t + 1)], axis=1)

    half = {}
    for b in range(2):
        for t, (r, col) in enumerate(TILES_LOW):
            tile = pair(lambda i: hown[b, i], t)
            if r == col:
                tile = tile * weight
            half[2 * b + r, 2 * b + col] = split(tile)
    for t, (r, col) in enumerate(TILES_ALL):
        half[2 + r, col] = split(pair(lambda i: cross[8 + i], t))

    def block(high, lowpart, r, col):
        rows, cols = slice(256 * r, 256 * r + 256), slice(256 * col, 256 * col + 256)
        return high[rows, cols], lowpart[rows, cols]

    for r in range(4):
        for col in range(r + 1):
            total = None
            for k in range(col, r + 1):
                part = dot3(block(wh, wl, r, k), half[k, col])
                total = part if total is None else total + part
            high, lowpart = split(total)
            mh[256 * r : 256 * r + 256, 256 * col : 256 * col + 256] = high
            ml[256 * r : 256 * r + 256, 256 * col : 256 * col + 256] = lowpart

    vmean = jnp.sum(s[0, 0, 128:136, :]) / (128 * CELLS)
    shift = jnp.where(rr == cc, vmean, 0.0)

    def product(r, col):
        total = None
        for k in range(min(r, col) + 1):
            part = dot3(block(mh, ml, r, k), block(wh, wl, col, k), NT)
            total = part if total is None else total + part
        return total

    for r in range(4):
        for col in range(r + 1):
            tile = product(r, col)
            if r == col:
                h_sub[256 * r : 256 * r + 256, 256 * r : 256 * r + 256] = tile + tile.T - shift
            else:
                tile = tile + product(col, r).T
                h_sub[256 * r : 256 * r + 256, 256 * col : 256 * col + 256] = tile
                h_sub[256 * col : 256 * col + 256, 256 * r : 256 * r + 256] = tile.T


def ham_kernel(orb, xlo, xhi, ylo, yhi, pot, hpsi, pay):
    row = lax.broadcasted_iota(jnp.int32, (128, 128), 0)
    col = lax.broadcasted_iota(jnp.int32, (128, 128), 1)
    away = (row - col + 128) % 128
    circle = jnp.where(
        away == 0,
        -90.0,
        jnp.where((away == 1) | (away == 127), 16.0, jnp.where((away == 2) | (away == 126), -1.0, 0.0)),
    ).astype(BF16)

    @pl.loop(0, 16)
    def _(step):
        rows = pl.ds(pl.multiple_of(step * 32, 32), 32)

        def slab(ref, i):
            return ref[rows, 128 * i : 128 * i + 128]

        def cell(a, b):
            if a < 0:
                return slab(xlo, (a + 2) * 4 + b)
            if a > 3:
                return slab(xhi, (a - 4) * 4 + b)
            if b < 0:
                return slab(ylo, a * 2 + b + 2)
            if b > 3:
                return slab(yhi, a * 2 + b - 4)
            return slab(orb, a * 4 + b)

        for a in range(4):
            for b in range(4):
                center = cell(a, b)
                lap = bdot(center, circle)
                field = lambda i, j: cell(i, j).astype(F32)
                near = field(a - 1, b) + field(a + 1, b) + field(a, b - 1) + field(a, b + 1)
                far = field(a - 2, b) + field(a + 2, b) + field(a, b - 2) + field(a, b + 2)
                lap = lap + (16.0 * near - far)
                level = pot[4 * a + b : 4 * a + b + 1, :]
                value = lap * (-0.5 / 12.0) + level * center.astype(F32)
                hpsi[rows, 128 * (4 * a + b) : 128 * (4 * a + b) + 128] = value.astype(BF16)

    for t, (r, c) in enumerate(TILES_LOW):
        tile = bdot(hpsi[256 * r : 256 * r + 256, :], orb[256 * c : 256 * c + 256, :], NT)
        pay[2 * t] = tile[:, :128]
        pay[2 * t + 1] = tile[:, 128:]


def cross_kernel(orb, hpsi, other, pay):
    for m, left in enumerate((orb, hpsi)):
        for t, (r, c) in enumerate(TILES_ALL):
            tile = bdot(left[256 * r : 256 * r + 256, :], other[256 * c : 256 * c + 256, :], NT)
            pay[8 * m + 2 * t] = tile[:, :128]
            pay[8 * m + 2 * t + 1] = tile[:, 128:]


def rotate_kernel(rot_other, rot_own, other, own, out):
    for i in range(4):
        cols = slice(512 * i, 512 * i + 512)
        total = bdot(rot_own[...], own[:, cols]) + bdot(rot_other[...], other[:, cols])
        out[:, cols] = total.astype(BF16)


def shifted(piece, distance):
    n = lax.axis_size("domain")
    return lax.ppermute(piece, "domain", [((i - distance) % n, i) for i in range(n)])


def y_shift(piece, distance):
    n = lax.axis_size("domain")
    route = [((i // 8) * 8 + (i % 8 - distance) % 8, i) for i in range(n)]
    return lax.ppermute(piece, "domain", route)


def shards(orbitals, potential):
    orb = orbitals.reshape(HALF, CELLS)
    pot = potential.reshape(16, 128)
    other = lax.ppermute(orb, "band", [(0, 1)])
    xlo = shifted(orb[:, 1024:], 8)
    xhi = shifted(orb[:, :1024], -8)
    ylo = y_shift(jnp.concatenate([orb[:, 512 * a + 256 : 512 * a + 512] for a in range(4)], axis=1), 1)
    yhi = y_shift(jnp.concatenate([orb[:, 512 * a : 512 * a + 256] for a in range(4)], axis=1), -1)

    slab = lambda n: jax.ShapeDtypeStruct((n, 256, 128), F32)
    square = lambda n, t: jax.ShapeDtypeStruct((n, n), t)
    s_pay = call(own_overlap_kernel, slab(6), (orb, pot), "own_overlap", flops=2 * 10**9)
    (s_sum,) = all_sum(s_pay, None, 0, "sum_own_overlap")
    w0 = call(first_factor_kernel, square(512, F32), (s_sum,), "first_factor", flops=40 * 10**9)
    hpsi, h_pay = call(
        ham_kernel,
        [jax.ShapeDtypeStruct((HALF, CELLS), BF16), slab(6)],
        (orb, xlo, xhi, ylo, yhi, pot),
        "hamiltonian",
        flops=10 * 10**9,
    )
    cross = call(cross_kernel, slab(16), (orb, hpsi, other), "cross_overlap", flops=4 * 10**9)
    h_sum, cross_sum = all_sum(h_pay, cross, 1, "sum_rest")
    h_sub, rot_other, rot_own = call(
        last_kernel,
        [square(1024, F32), square(512, BF16), square(512, BF16)],
        (s_sum, h_sum, cross_sum, w0),
        "last_factor",
        scratch=[
            pltpu.VMEM((512, 1024), F32),
            pltpu.VMEM((512, 512), F32),
            pltpu.VMEM((1024, 1024), BF16),
            pltpu.VMEM((1024, 1024), BF16),
            pltpu.VMEM((1024, 1024), BF16),
            pltpu.VMEM((1024, 1024), BF16),
        ],
        flops=50 * 10**9,
    )
    rotated = call(
        rotate_kernel,
        jax.ShapeDtypeStruct((HALF, CELLS), BF16),
        (rot_other, rot_own, other, orb),
        "rotate",
        flops=4 * 10**9,
    )
    return rotated.reshape(orbitals.shape), h_sub


def solution(mesh):
    in_specs = (P("band", "domain", None), P("domain", None))
    out_specs = (P("band", "domain", None), P())
    return jax.shard_map(shards, mesh=mesh, in_specs=in_specs, out_specs=out_specs, check_vma=False)
```

```python
import jax
import jax.numpy as jnp
from jax import lax
from jax.experimental import pallas as pl
from jax.experimental.pallas import tpu as pltpu
from jax.sharding import PartitionSpec as P

MESH = pl.DeviceIdType.MESH
HI = lax.Precision.HIGHEST
NN = (((1,), (0,)), ((), ()))
NT = (((1,), (1,)), ((), ()))
TN = (((0,), (0,)), ((), ()))
F32 = jnp.float32
BF16 = jnp.bfloat16
VMEM = pl.BlockSpec(memory_space=pltpu.VMEM)
ANY = pl.BlockSpec(memory_space=pl.ANY)
MIB = 2**20
CELLS = 2048
HALF = 512
TILES_UP = ((0, 0), (0, 1), (1, 1))
TILES_LOW = ((0, 0), (1, 0), (1, 1))
TILES_ALL = ((0, 0), (0, 1), (1, 0), (1, 1))


def fdot(a, b, dims=NN):
    return lax.dot_general(a, b, dims, precision=HI, preferred_element_type=F32)


def bdot(a, b, dims=NN):
    return lax.dot_general(a, b, dims, preferred_element_type=F32)


def call(kernel, outs, args, name, scratch=(), collective=None, limit=48, flops=0, far_in=(), far_out=()):
    params = dict(vmem_limit_bytes=limit * MIB)
    if collective is not None:
        params.update(collective_id=collective, has_side_effects=True)
    return pl.pallas_call(
        kernel,
        out_shape=outs,
        in_specs=[ANY if i in far_in else VMEM for i in range(len(args))],
        out_specs=[ANY if i in far_out else VMEM for i in range(len(outs))],
        scratch_shapes=list(scratch),
        compiler_params=pltpu.CompilerParams(**params),
        cost_estimate=pl.CostEstimate(flops=flops, bytes_accessed=8 * MIB, transcendentals=0),
        name=name,
    )(*args)


def packers(lower):
    z = lax.broadcasted_iota(jnp.int32, (128, 128), 0)
    lane = lax.broadcasted_iota(jnp.int32, (128, 128), 1)
    even = (lane < 64) & (z == lane + lower)
    odd = (lane >= 64) & (z == lane - 64 + lower)
    return even.astype(F32).astype(BF16), odd.astype(F32).astype(BF16)


def edge_cells():
    lane = lax.broadcasted_iota(jnp.int32, (128, 128), 1)
    q = lane % 4
    return lane // 4, jnp.where(q < 2, 64 + q, 124 + q)


def pack_kernel(orb, pot, pay, send, keep):
    band = lax.axis_index("band")
    for t, (r, c) in enumerate(TILES_UP):
        tile = bdot(orb[256 * r : 256 * r + 256, :], orb[256 * c : 256 * c + 256, :], NT)
        pay[2 * t] = tile[:, :128]
        pay[2 * t + 1] = tile[:, 128:]
    pay[0, 128:136, :] = pot[0:8, :] + pot[8:16, :]
    z = lax.broadcasted_iota(jnp.int32, (128, 128), 0)
    owner, level = edge_cells()

    @pl.loop(0, 4)
    def _(step):
        rows = pl.ds(pl.multiple_of(step * 128, 128), 128)
        slab = lambda i: orb[rows, 128 * i : 128 * i + 128]
        for ref, lower in ((send, 64 * band), (keep, 64 - 64 * band)):
            even, odd = packers(lower)
            for m in range(8):
                packed = bdot(slab(2 * m), even) + bdot(slab(2 * m + 1), odd)
                ref[rows, 128 * m : 128 * m + 128] = packed.astype(BF16)
        edge = jnp.zeros((128, 128), F32)
        for i in range(16):
            pick = ((owner == i) & (z == level)).astype(F32).astype(BF16)
            edge = edge + bdot(slab(i), pick)
        send[rows, 1024:1152] = edge.astype(BF16)


class Place:
    def __init__(self):
        self.band = lax.axis_index("band")
        dom = lax.axis_index("domain")
        self.x, self.y = dom // 32, (dom // 8) % 4
        self.z, self.core = (dom // 2) % 4, dom % 2
        self.here = self.x * 4 + self.y
        self.zz = self.band * 4 + self.z
        self.partner = self.at(self.band, self.x, self.y, self.z, 1 - self.core)
        self.opposite = (1 - self.band, dom)
        self.next_x = (self.band, (dom + 8) % 128)
        self.last_x = (self.band, (dom + 120) % 128)
        self.next_y = (self.band, (dom // 8) * 8 + (dom + 1) % 8)
        self.last_y = (self.band, (dom // 8) * 8 + (dom + 7) % 8)

    @staticmethod
    def at(b, xx, yy, zl, cc):
        return (b, ((xx * 4 + yy) * 4 + zl) * 2 + cc)

    def xy_peer(self, k):
        xx, yy = (self.x + k // 4) % 4, (self.y + k % 4) % 4
        return self.at(self.band, xx, yy, self.z, self.core), xx * 4 + yy

    def xy_source(self, k):
        return ((self.x + 4 - k // 4) % 4) * 4 + (self.y + 4 - k % 4) % 4

    def z_peer(self, k):
        other = (self.zz + k) % 8
        return self.at(other // 4, self.x, self.y, other % 4, self.core)

    def greet(self, y_too):
        barrier = pltpu.get_barrier_semaphore()
        peers = [self.partner]
        peers += [self.xy_peer(k)[0] for k in range(1, 16)]
        peers += [self.z_peer(k) for k in range(1, 8)]
        if y_too:
            band, dom = self.next_y
            peers.append((band, jnp.where(self.core == 0, self.last_y[1], dom)))
        for peer in peers:
            pl.semaphore_signal(barrier, inc=1, device_id=peer, device_id_type=MESH)
        pl.semaphore_wait(barrier, len(peers))


def remote(src, dst, send, recv, device):
    return pltpu.make_async_remote_copy(
        src_ref=src, dst_ref=dst, send_sem=send, recv_sem=recv, device_id=device, device_id_type=MESH
    )


class Bulk:
    def __init__(self, pieces, device, sems, first, condition=None, other=None):
        self.sems, self.first, self.device = sems, first, device
        self.pieces, self.condition, self.other = pieces, condition, other
        self.started = 0

    def copy(self, i):
        src, dst = self.pieces[i]
        return remote(src, dst, self.sems[0].at[self.first + i], self.sems[1].at[self.first + i], self.device)

    def start(self, count=None):
        stop = len(self.pieces) if count is None else self.started + count

        def body():
            for i in range(self.started, stop):
                self.copy(i).start()

        if self.condition is None:
            body()
        else:
            pl.when(self.condition)(body)
        self.started = stop

    def wait(self):
        if self.condition is None:
            for i in range(len(self.pieces)):
                self.copy(i).wait()
            return

        @pl.when(self.condition)
        def _():
            for i in range(len(self.pieces)):
                self.copy(i).wait_send()

        @pl.when(self.other)
        def _():
            for i in range(len(self.pieces)):
                self.copy(i).wait_recv()


class Sum:
    scratch_count = 4 + 10

    def __init__(self, place, both, pay, out, scratch):
        self.place, self.both, self.pay, self.out = place, both, pay, out
        self.half, self.whole, self.got, self.along = scratch[:4]
        self.s1, self.r1, self.s2, self.r2, self.s3, self.r3, self.s4, self.r4, self.s5, self.r5 = scratch[4:14]

    @staticmethod
    def scratch(n):
        dma = pltpu.SemaphoreType.DMA
        return [
            pltpu.VMEM((n, 128, 128), F32),
            pltpu.VMEM((n, 128, 128), F32),
            pltpu.VMEM((16, n, 8, 128), F32),
            pltpu.VMEM((8, n, 8, 128), F32),
            dma((1,)),
            dma((1,)),
            dma((16,)),
            dma((16,)),
            dma((8,)),
            dma((8,)),
            dma((16,)),
            dma((16,)),
            dma((16,)),
            dma((16,)),
        ]

    def first(self):
        p = self.place
        theirs = pl.ds(pl.multiple_of((1 - p.core) * 128, 128), 128)
        return remote(self.pay.at[:, theirs, :], self.half, self.s1.at[0], self.r1.at[0], p.partner)

    def second(self, k):
        device, there = self.place.xy_peer(k)
        rows = pl.ds(pl.multiple_of(there * 8, 8), 8)
        return remote(self.whole.at[:, rows, :], self.got.at[k], self.s2.at[k], self.r2.at[k], device)

    def third(self, k):
        p = self.place
        return remote(self.along.at[p.zz], self.along.at[p.zz], self.s3.at[k], self.r3.at[k], p.z_peer(k))

    def spot(self, row):
        rows = pl.ds(pl.multiple_of(self.place.core * 128 + row * 8, 8), 8)
        return self.out.at[:, :, rows, :] if self.both else self.out.at[:, rows, :]

    def fourth(self, k, row):
        spot = self.spot(row)
        return remote(spot, spot, self.s4.at[k], self.r4.at[k], self.place.xy_peer(k)[0])

    def fifth(self, k, row):
        spot = self.spot(row)
        return remote(spot, spot, self.s5.at[k], self.r5.at[k], self.place.partner)

    def part1(self):
        self.first().start()

    def part2(self):
        self.first().wait()
        mine = pl.ds(pl.multiple_of(self.place.core * 128, 128), 128)
        self.whole[...] = self.pay[:, mine, :] + self.half[...]
        for k in range(1, 16):
            self.second(k).start()

    def part3(self):
        p = self.place
        for k in range(1, 16):
            self.second(k).wait()
        total = self.whole[:, pl.ds(pl.multiple_of(p.here * 8, 8), 8), :]
        for k in range(1, 16):
            total = total + self.got[k]
        self.along[p.zz] = total
        for k in range(1, 8):
            self.third(k).start()

    def part4(self):
        p = self.place
        for k in range(1, 8):
            self.third(k).wait()
        along = self.along
        lower = along[0] + along[1] + along[2] + along[3]
        upper = along[4] + along[5] + along[6] + along[7]
        rows = pl.ds(pl.multiple_of(p.core * 128 + p.here * 8, 8), 8)
        if self.both:
            self.out[0, :, rows, :] = lower
            self.out[1, :, rows, :] = upper
        else:
            self.out[:, rows, :] = lower + upper
        for k in range(1, 16):
            self.fourth(k, p.here).start()
        self.fifth(0, p.here).start()

    def part5(self):
        p = self.place
        for k in range(1, 16):
            source = p.xy_source(k)
            self.fourth(k, source).wait_recv()
            self.fifth(k, source).start()

    def end(self):
        p = self.place
        for k in range(1, 16):
            self.fourth(k, p.here).wait_send()
        for k in range(16):
            self.fifth(k, p.here).wait()


def invert_block(block):
    lane = lax.broadcasted_iota(jnp.int32, (8, 128), 1)
    sub = lax.broadcasted_iota(jnp.int32, (8, 128), 0)
    rows = [block[8 * p : 8 * p + 8] for p in range(16)]
    for p in range(16):
        k = 8 * p
        panel = rows[p]
        d = [[jnp.broadcast_to(panel[i : i + 1, k + j : k + j + 1], (8, 128)) for j in range(i + 1)] for i in range(8)]
        inside = (lane >= k) & (lane < k + 8)
        start = jnp.where(inside, (lane == k + sub).astype(F32), panel)
        acc = [jnp.broadcast_to(start[s : s + 1, :], (8, 128)) for s in range(8)]
        done = []
        for j in range(8):
            r = lax.rsqrt(d[j][j])
            xj = acc[j] * r
            done.append(xj)
            low = [None] * 8
            for i in range(j + 1, 8):
                low[i] = d[i][j] * r
            for i in range(j + 1, 8):
                for m in range(j + 1, i + 1):
                    d[i][m] = d[i][m] - low[i] * low[m]
                acc[i] = acc[i] - low[i] * xj
        x = done[0]
        for s in range(1, 8):
            x = jnp.where(sub == s, done[s], x)
        rows[p] = x
        if p < 15:
            right = jnp.where(lane >= k + 8, x, 0.0)
            update = fdot(right, x, TN)
            for q in range(p + 1, 16):
                rows[q] = jnp.where(inside, 0.0, rows[q]) - update[8 * q : 8 * q + 8]
    whole = jnp.concatenate(rows, axis=0)
    rr = lax.broadcasted_iota(jnp.int32, (128, 128), 0)
    cc = lax.broadcasted_iota(jnp.int32, (128, 128), 1)
    return jnp.where(cc <= rr, whole, 0.0)


def eliminate_step(c, offset, j):
    blocks = c.shape[0] // 128
    rr = lax.broadcasted_iota(jnp.int32, (128, 128), 0)
    cc = lax.broadcasted_iota(jnp.int32, (128, 128), 1)
    rows, cols = slice(128 * j, 128 * j + 128), slice(offset + 128 * j, offset + 128 * j + 128)
    inverse = invert_block(c[rows, cols])
    c[rows, cols] = (rr == cc).astype(F32)
    c[rows, :] = fdot(inverse, c[rows, :])
    for i in range(j + 1, blocks):
        below = slice(128 * i, 128 * i + 128)
        across = slice(offset + 128 * i, offset + 128 * i + 128)
        factor = c[rows, across]
        c[below, cols] = jnp.zeros((128, 128), F32)
        c[below, :] = c[below, :] - fdot(factor, c[rows, :], TN)


def clear_right(c, offset):
    for i in range(c.shape[0] // 128):
        for j in range(i + 1, c.shape[0] // 128):
            c[128 * i : 128 * i + 128, offset + 128 * j : offset + 128 * j + 128] = jnp.zeros((128, 128), F32)


def spread(c, slabs, tiles, offset):
    for t, (r, col) in enumerate(tiles):
        for h in range(2):
            lo = offset + 256 * col + 128 * h
            c[256 * r : 256 * r + 256, lo : lo + 128] = slabs(2 * t + h)


def swap_kernel(pay, orb, send, s_sum, recv, xlo, xhi, *scratch):
    place = Place()
    total = Sum(place, True, pay, s_sum, scratch[:14])
    sems = scratch[14:16]
    rows = lambda n, i: pl.ds((HALF // n) * i, HALF // n)
    swap = Bulk([(send.at[rows(8, i), :], recv.at[rows(8, i), :]) for i in range(8)], place.opposite, sems, 0)
    up = Bulk(
        [(orb.at[rows(4, i), pl.ds(1024, 1024)], xlo.at[rows(4, i), :]) for i in range(4)], place.next_x, sems, 8
    )
    down = Bulk(
        [(orb.at[rows(4, i), pl.ds(0, 1024)], xhi.at[rows(4, i), :]) for i in range(4)], place.last_x, sems, 12
    )
    place.greet(False)
    total.part1()
    swap.start(2)
    total.part2()
    up.start()
    down.start()
    total.part3()
    swap.start()
    total.part4()
    total.part5()
    total.end()
    up.wait()
    down.wait()
    swap.wait()


def first_factor_kernel(s, pay, orb, x_sum, w, ylo, yhi, *scratch):
    place = Place()
    total = Sum(place, False, pay, x_sum, scratch[:14])
    sems = scratch[14:16]
    up = Bulk(
        [(orb.at[:, pl.ds(512 * a + 256, 256)], ylo.at[:, pl.ds(256 * a, 256)]) for a in range(4)],
        place.next_y,
        sems,
        0,
    )
    down = Bulk(
        [(orb.at[:, pl.ds(512 * a, 256)], yhi.at[:, pl.ds(256 * a, 256)]) for a in range(4)], place.last_y, sems, 4
    )
    place.greet(True)
    total.part1()
    w[256:512, 0:256] = jnp.zeros((256, 256), F32)
    spread(w, lambda i: s[0, i], TILES_UP, 0)
    total.part2()
    eliminate_step(w, 0, 0)
    total.part3()
    up.start()
    down.start()
    eliminate_step(w, 0, 1)
    total.part4()
    eliminate_step(w, 0, 2)
    total.part5()
    eliminate_step(w, 0, 3)
    clear_right(w, 0)
    total.end()
    up.wait()
    down.wait()


def second_factor_kernel(s, x, w0, hown, hcross, keep, c, hown_sum, hcross_sum, rest, *scratch):
    place = Place()
    own = Sum(place, True, hown, hown_sum, scratch[:14])
    cross = Sum(place, False, hcross, hcross_sum, scratch[14:28])
    sems = scratch[28:30]
    cross_s = scratch[30]
    rows = lambda i: pl.ds(64 * i, 64)
    tail = Bulk(
        [(keep.at[rows(i), :], rest.at[rows(i), :]) for i in range(8)],
        place.opposite,
        sems,
        0,
        place.band == 0,
        place.band == 1,
    )
    place.greet(False)
    own.part1()
    cross.part1()
    for t, (r, col) in enumerate(TILES_ALL):
        for h in range(2):
            lo = 256 * col + 128 * h
            cross_s[256 * r : 256 * r + 256, lo : lo + 128] = x[2 * t + h]
    low = fdot(cross_s[...], w0[...], NT)
    c[256:512, 512:768] = jnp.zeros((256, 256), F32)
    spread(c, lambda i: s[1, i], TILES_UP, 512)
    c[:, 512:1024] = c[:, 512:1024] - fdot(low, low, NT)
    c[:, 0:512] = -fdot(low, w0[...])
    own.part2()
    cross.part2()
    eliminate_step(c, 512, 0)
    own.part3()
    cross.part3()
    tail.start()
    eliminate_step(c, 512, 1)
    own.part4()
    cross.part4()
    eliminate_step(c, 512, 2)
    own.part5()
    cross.part5()
    eliminate_step(c, 512, 3)
    clear_right(c, 512)
    own.end()
    cross.end()
    tail.wait()


def split(a):
    high = a.astype(BF16)
    return high, (a - high.astype(F32)).astype(BF16)


def dot3(a, b, dims=NN):
    return bdot(a[0], b[0], dims) + (bdot(a[0], b[1], dims) + bdot(a[1], b[0], dims))


def last_kernel(s, hown, cross, w0, c, h_sub, rot_other, rot_own, wh, wl, mh, ml):
    band = lax.axis_index("band")

    @pl.when(band == 0)
    def _():
        rot_own[...] = w0[...].astype(BF16)
        rot_other[...] = jnp.zeros((512, 512), BF16)

    @pl.when(band == 1)
    def _():
        rot_own[...] = c[:, 512:1024].astype(BF16)
        rot_other[...] = c[:, 0:512].astype(BF16)

    for r in range(4):
        source = w0 if r < 2 else c
        base = 256 * (r % 2)
        width = 512 if r < 2 else 1024
        high, lowpart = split(source[base : base + 256, :])
        wh[256 * r : 256 * r + 256, 0:width] = high
        wl[256 * r : 256 * r + 256, 0:width] = lowpart

    rr = lax.broadcasted_iota(jnp.int32, (256, 256), 0)
    cc = lax.broadcasted_iota(jnp.int32, (256, 256), 1)
    weight = jnp.where(cc < rr, 1.0, jnp.where(cc == rr, 0.5, 0.0)).astype(F32)

    def pair(slabs, t):
        return jnp.concatenate([slabs(2 * t), slabs(2 * t + 1)], axis=1)

    half = {}
    for b in range(2):
        for t, (r, col) in enumerate(TILES_LOW):
            tile = pair(lambda i: hown[b, i], t)
            if r == col:
                tile = tile * weight
            half[2 * b + r, 2 * b + col] = split(tile)
    for t, (r, col) in enumerate(TILES_ALL):
        half[2 + r, col] = split(pair(lambda i: cross[i], t))

    def block(high, lowpart, r, col):
        rows, cols = slice(256 * r, 256 * r + 256), slice(256 * col, 256 * col + 256)
        return high[rows, cols], lowpart[rows, cols]

    for r in range(4):
        for col in range(r + 1):
            total = None
            for k in range(col, r + 1):
                part = dot3(block(wh, wl, r, k), half[k, col])
                total = part if total is None else total + part
            high, lowpart = split(total)
            mh[256 * r : 256 * r + 256, 256 * col : 256 * col + 256] = high
            ml[256 * r : 256 * r + 256, 256 * col : 256 * col + 256] = lowpart

    vmean = jnp.sum(s[0, 0, 128:136, :]) / (128 * CELLS)
    shift = jnp.where(rr == cc, vmean, 0.0)

    def product(r, col):
        total = None
        for k in range(min(r, col) + 1):
            part = dot3(block(mh, ml, r, k), block(wh, wl, col, k), NT)
            total = part if total is None else total + part
        return total

    for r in range(4):
        for col in range(r + 1):
            tile = product(r, col)
            if r == col:
                h_sub[256 * r : 256 * r + 256, 256 * r : 256 * r + 256] = tile + tile.T - shift
            else:
                tile = tile + product(col, r).T
                h_sub[256 * r : 256 * r + 256, 256 * col : 256 * col + 256] = tile
                h_sub[256 * col : 256 * col + 256, 256 * r : 256 * r + 256] = tile.T


def circle_weights():
    row = lax.broadcasted_iota(jnp.int32, (128, 128), 0)
    col = lax.broadcasted_iota(jnp.int32, (128, 128), 1)
    return row, col, step_weights((row - col + 128) % 128)


def step_weights(away):
    near = (away == 1) | (away == 127)
    far = (away == 2) | (away == 126)
    return jnp.where(near, 16.0, jnp.where(far, -1.0, 0.0))


def ham_kernel(orb, xlo, xhi, ylo, yhi, pot, recv, pay, cross, hpsi, half, edge):
    band = lax.axis_index("band")
    row, col, weights = circle_weights()
    full = jnp.where(row == col, -90.0, weights)
    inner = jnp.where((band == 1) | ((row >= 64) & (col >= 64)), full, 0.0)
    full, inner = full.astype(BF16), inner.astype(BF16)
    owner, level = edge_cells()
    even, odd = packers(64 - 64 * band)

    @pl.loop(0, 16)
    def _(step):
        rows = pl.ds(pl.multiple_of(step * 32, 32), 32)

        def slab(ref, i):
            return ref[rows, 128 * i : 128 * i + 128]

        def cell(a, b):
            if a < 0:
                return slab(xlo, (a + 2) * 4 + b)
            if a > 3:
                return slab(xhi, (a - 4) * 4 + b)
            if b < 0:
                return slab(ylo, a * 2 + b + 2)
            if b > 3:
                return slab(yhi, a * 2 + b - 4)
            return slab(orb, a * 4 + b)

        for pair in range(8):
            packed = None
            for i in (2 * pair, 2 * pair + 1):
                a, b = i // 4, i % 4
                center = cell(a, b)
                field = lambda i, j: cell(i, j).astype(F32)
                near = field(a - 1, b) + field(a + 1, b) + field(a, b - 1) + field(a, b + 1)
                far = field(a - 2, b) + field(a + 2, b) + field(a, b - 2) + field(a, b + 2)
                across = 16.0 * near - far
                base = pot[i : i + 1, :] * center.astype(F32)
                value = (across + bdot(center, full)) * (-0.5 / 12.0) + base
                hpsi[rows, 128 * i : 128 * i + 128] = value.astype(BF16)
                value = (across + bdot(center, inner)) * (-0.5 / 12.0) + base
                part = bdot(value.astype(BF16), even if i % 2 == 0 else odd)
                packed = part if packed is None else packed + part
            half[rows, 128 * pair : 128 * pair + 128] = packed.astype(BF16)

    @pl.loop(0, 4)
    def _(step):
        rows = pl.ds(pl.multiple_of(step * 128, 128), 128)
        total = jnp.zeros((128, 128), F32)
        for i in range(16):
            weight = jnp.where((owner == i) & (row < 64), step_weights((row - level + 128) % 128), 0.0)
            total = total + bdot(orb[rows, 128 * i : 128 * i + 128], weight.astype(BF16))
        edge[rows, :] = jnp.where(band == 1, total * (-0.5 / 12.0), 0.0).astype(BF16)

    for t, (r, c) in enumerate(TILES_LOW):
        tile = bdot(hpsi[256 * r : 256 * r + 256, :], orb[256 * c : 256 * c + 256, :], NT)
        pay[2 * t] = tile[:, :128]
        pay[2 * t + 1] = tile[:, 128:]
    cross_products(band, half, recv, cross, edge)


def cross_products(band, half, recv, out, edge=None):
    def products(left, right, corner):
        for t, (r, c) in enumerate(TILES_ALL):
            up, across = slice(256 * r, 256 * r + 256), slice(256 * c, 256 * c + 256)
            tile = bdot(left[up, 0:1024], right[across, 0:1024], NT)
            if corner:
                tile = tile + bdot(edge[up, :], recv[across, 1024:1152], NT)
            out[2 * t] = tile[:, :128]
            out[2 * t + 1] = tile[:, 128:]

    @pl.when(band == 1)
    def _():
        products(half, recv, edge is not None)

    @pl.when(band == 0)
    def _():
        products(recv, half, False)


def cross_kernel(keep, recv, out):
    cross_products(lax.axis_index("band"), keep, recv, out)


def rotate_kernel(rot_other, rot_own, recv, rest, own, out):
    band = lax.axis_index("band")

    @pl.when(band == 0)
    def _():
        for i in range(4):
            there = slice(512 * i, 512 * i + 512)
            out[:, there] = bdot(rot_own[...], own[:, there]).astype(BF16)

    @pl.when(band == 1)
    def _():
        low_even, low_odd = packers(0)
        high_even, high_odd = packers(64)
        for m in range(8):
            cols = slice(128 * m, 128 * m + 128)
            low, high = recv[:, cols], rest[:, cols]
            even = (bdot(low, low_even, NT) + bdot(high, high_even, NT)).astype(BF16)
            odd = (bdot(low, low_odd, NT) + bdot(high, high_odd, NT)).astype(BF16)
            other = jnp.concatenate([even, odd], axis=1)
            there = slice(256 * m, 256 * m + 256)
            total = bdot(rot_own[...], own[:, there]) + bdot(rot_other[...], other)
            out[:, there] = total.astype(BF16)


def shards(orbitals, potential):
    orb = orbitals.reshape(HALF, CELLS)
    pot = potential.reshape(16, 128)
    slab = lambda n: jax.ShapeDtypeStruct((n, 256, 128), F32)
    square = lambda n, t: jax.ShapeDtypeStruct((n, n), t)
    wide = lambda n: jax.ShapeDtypeStruct((HALF, n), BF16)
    two = lambda n: jax.ShapeDtypeStruct((2, n, 256, 128), F32)
    dma = pltpu.SemaphoreType.DMA
    s_pay, send, keep = call(pack_kernel, [slab(6), wide(1152), wide(1024)], (orb, pot), "pack")
    s_sum, recv, xlo, xhi = call(
        swap_kernel,
        [two(6), wide(1152), wide(1024), wide(1024)],
        (s_pay, orb, send),
        "swap_and_sum",
        scratch=Sum.scratch(6) + [dma((16,)), dma((16,))],
        collective=0,
        far_in=(1, 2),
        far_out=(1, 2, 3),
    )
    (x_pay,) = call(cross_kernel, [slab(8)], (keep, recv), "cross_overlap")
    x_sum, w0, ylo, yhi = call(
        first_factor_kernel,
        [slab(8), square(512, F32), wide(1024), wide(1024)],
        (s_sum, x_pay, orb),
        "first_factor",
        scratch=Sum.scratch(8) + [dma((8,)), dma((8,))],
        collective=1,
        far_in=(2,),
        far_out=(2, 3),
    )
    h_pay, hx_pay = call(
        ham_kernel,
        [slab(6), slab(8)],
        (orb, xlo, xhi, ylo, yhi, pot, recv),
        "hamiltonian",
        scratch=[pltpu.VMEM((HALF, CELLS), BF16), pltpu.VMEM((HALF, 1024), BF16), pltpu.VMEM((HALF, 128), BF16)],
    )
    c, h_sum, hx_sum, rest = call(
        second_factor_kernel,
        [jax.ShapeDtypeStruct((HALF, 1024), F32), two(6), slab(8), wide(1024)],
        (s_sum, x_sum, w0, h_pay, hx_pay, keep),
        "second_factor",
        scratch=Sum.scratch(6) + Sum.scratch(8) + [dma((8,)), dma((8,)), pltpu.VMEM((512, 512), F32)],
        collective=2,
        far_in=(5,),
        far_out=(3,),
    )
    h_sub, rot_other, rot_own = call(
        last_kernel,
        [square(1024, F32), square(512, BF16), square(512, BF16)],
        (s_sum, h_sum, hx_sum, w0, c),
        "subspace_matrix",
        scratch=[pltpu.VMEM((1024, 1024), BF16)] * 4,
    )
    (rotated,) = call(rotate_kernel, [wide(CELLS)], (rot_other, rot_own, recv, rest, orb), "rotate")
    return rotated.reshape(orbitals.shape), h_sub


def solution(mesh):
    in_specs = (P("band", "domain", None), P("domain", None))
    out_specs = (P("band", "domain", None), P())
    return jax.shard_map(shards, mesh=mesh, in_specs=in_specs, out_specs=out_specs, check_vma=False)
```

```python
import jax
import jax.numpy as jnp
from jax import lax
from jax.experimental import pallas as pl
from jax.experimental.pallas import tpu as pltpu
from jax.sharding import PartitionSpec as P

MESH = pl.DeviceIdType.MESH
HI = lax.Precision.HIGHEST
NN = (((1,), (0,)), ((), ()))
NT = (((1,), (1,)), ((), ()))
TN = (((0,), (0,)), ((), ()))
F32 = jnp.float32
BF16 = jnp.bfloat16
VMEM = pl.BlockSpec(memory_space=pltpu.VMEM)
ANY = pl.BlockSpec(memory_space=pl.ANY)
MIB = 2**20
CELLS = 2048
HALF = 512
TILES_UP = ((0, 0), (0, 1), (1, 1))
TILES_LOW = ((0, 0), (1, 0), (1, 1))
TILES_ALL = ((0, 0), (0, 1), (1, 0), (1, 1))


def fdot(a, b, dims=NN):
    return lax.dot_general(a, b, dims, precision=HI, preferred_element_type=F32)


def bdot(a, b, dims=NN):
    return lax.dot_general(a, b, dims, preferred_element_type=F32)


def call(kernel, outs, args, name, scratch=(), collective=None, limit=48, flops=0, far_in=(), far_out=()):
    params = dict(vmem_limit_bytes=limit * MIB)
    if collective is not None:
        params.update(collective_id=collective, has_side_effects=True)
    return pl.pallas_call(
        kernel,
        out_shape=outs,
        in_specs=[ANY if i in far_in else VMEM for i in range(len(args))],
        out_specs=[ANY if i in far_out else VMEM for i in range(len(outs))],
        scratch_shapes=list(scratch),
        compiler_params=pltpu.CompilerParams(**params),
        cost_estimate=pl.CostEstimate(flops=flops, bytes_accessed=8 * MIB, transcendentals=0),
        name=name,
    )(*args)


def packers(lower):
    z = lax.broadcasted_iota(jnp.int32, (128, 128), 0)
    lane = lax.broadcasted_iota(jnp.int32, (128, 128), 1)
    even = (lane < 64) & (z == lane + lower)
    odd = (lane >= 64) & (z == lane - 64 + lower)
    return even.astype(F32).astype(BF16), odd.astype(F32).astype(BF16)


def edge_cells():
    lane = lax.broadcasted_iota(jnp.int32, (128, 128), 1)
    q = lane % 4
    return lane // 64, (lane % 64) // 4, jnp.where(q < 2, 64 + q, 124 + q)


def pack(band, orb, pot, pay, send, keep, edge_send):
    for t, (r, c) in enumerate(TILES_UP):
        tile = bdot(orb[256 * r : 256 * r + 256, :], orb[256 * c : 256 * c + 256, :], NT)
        pay[2 * t] = tile[:, :128]
        pay[2 * t + 1] = tile[:, 128:]
    pay[0, 128:136, :] = pot[0:8, :] + pot[8:16, :]
    z = lax.broadcasted_iota(jnp.int32, (128, 128), 0)
    side, owner, level = edge_cells()

    @pl.loop(0, 4)
    def _(step):
        rows = pl.ds(pl.multiple_of(step * 128, 128), 128)
        slab = lambda i: orb[rows, 128 * i : 128 * i + 128]
        for ref, lower in ((send, 64 * band), (keep, 64 - 64 * band)):
            even, odd = packers(lower)
            for m in range(8):
                packed = bdot(slab(2 * m), even) + bdot(slab(2 * m + 1), odd)
                ref[rows, 128 * m : 128 * m + 128] = packed.astype(BF16)

    @pl.loop(0, 2)
    def _(step):
        edge = jnp.zeros((128, 128), F32)
        for h in range(2):
            rows = pl.ds(pl.multiple_of(step * 128, 128) + 256 * h, 128)
            for i in range(16):
                pick = ((side == h) & (owner == i) & (z == level)).astype(F32).astype(BF16)
                edge = edge + bdot(orb[rows, 128 * i : 128 * i + 128], pick)
        edge_send[pl.ds(pl.multiple_of(step * 128, 128), 128), :] = edge.astype(BF16)


class Place:
    def __init__(self):
        self.band = lax.axis_index("band")
        dom = lax.axis_index("domain")
        self.x, self.y = dom // 32, (dom // 8) % 4
        self.z, self.core = (dom // 2) % 4, dom % 2
        self.here = self.x * 4 + self.y
        self.zz = self.band * 4 + self.z
        self.partner = self.at(self.band, self.x, self.y, self.z, 1 - self.core)
        self.opposite = (1 - self.band, dom)
        self.next_x = (self.band, (dom + 8) % 128)
        self.last_x = (self.band, (dom + 120) % 128)
        self.next_y = (self.band, (dom // 8) * 8 + (dom + 1) % 8)
        self.last_y = (self.band, (dom // 8) * 8 + (dom + 7) % 8)

    @staticmethod
    def at(b, xx, yy, zl, cc):
        return (b, ((xx * 4 + yy) * 4 + zl) * 2 + cc)

    def xy_peer(self, k):
        xx, yy = (self.x + k // 4) % 4, (self.y + k % 4) % 4
        return self.at(self.band, xx, yy, self.z, self.core), xx * 4 + yy

    def xy_source(self, k):
        return ((self.x + 4 - k // 4) % 4) * 4 + (self.y + 4 - k % 4) % 4

    def z_peer(self, k):
        other = (self.zz + k) % 8
        return self.at(other // 4, self.x, self.y, other % 4, self.core)

    def greet(self, y_too):
        barrier = pltpu.get_barrier_semaphore()
        peers = [self.partner]
        peers += [self.xy_peer(k)[0] for k in range(1, 16)]
        peers += [self.z_peer(k) for k in range(1, 8)]
        if y_too:
            band, dom = self.next_y
            peers.append((band, jnp.where(self.core == 0, self.last_y[1], dom)))
        for peer in peers:
            pl.semaphore_signal(barrier, inc=1, device_id=peer, device_id_type=MESH)
        pl.semaphore_wait(barrier, len(peers))


def remote(src, dst, send, recv, device):
    return pltpu.make_async_remote_copy(
        src_ref=src, dst_ref=dst, send_sem=send, recv_sem=recv, device_id=device, device_id_type=MESH
    )


class Bulk:
    def __init__(self, pieces, device, sems, first, condition=None, other=None):
        self.sems, self.first, self.device = sems, first, device
        self.pieces, self.condition, self.other = pieces, condition, other
        self.started = 0

    def copy(self, i):
        src, dst = self.pieces[i]
        return remote(src, dst, self.sems[0].at[self.first + i], self.sems[1].at[self.first + i], self.device)

    def start(self, count=None):
        stop = len(self.pieces) if count is None else self.started + count

        def body():
            for i in range(self.started, stop):
                self.copy(i).start()

        if self.condition is None:
            body()
        else:
            pl.when(self.condition)(body)
        self.started = stop

    def wait(self):
        if self.condition is None:
            for i in range(len(self.pieces)):
                self.copy(i).wait()
            return

        @pl.when(self.condition)
        def _():
            for i in range(len(self.pieces)):
                self.copy(i).wait_send()

        @pl.when(self.other)
        def _():
            for i in range(len(self.pieces)):
                self.copy(i).wait_recv()


class Sum:
    scratch_count = 4 + 10

    def __init__(self, place, both, pay, out, scratch):
        self.place, self.both, self.pay, self.out = place, both, pay, out
        self.side = pay.shape[1] // 2
        self.part = self.side // 16
        self.half, self.whole, self.got, self.along = scratch[:4]
        self.s1, self.r1, self.s2, self.r2, self.s3, self.r3, self.s4, self.r4, self.s5, self.r5 = scratch[4:14]

    @staticmethod
    def scratch(n, height=256, wire=F32):
        dma = pltpu.SemaphoreType.DMA
        return [
            pltpu.VMEM((n, height // 2, 128), wire),
            pltpu.VMEM((n, height // 2, 128), wire),
            pltpu.VMEM((16, n, height // 32, 128), wire),
            pltpu.VMEM((8, n, height // 32, 128), wire),
            dma((1,)),
            dma((1,)),
            dma((16,)),
            dma((16,)),
            dma((8,)),
            dma((8,)),
            dma((16,)),
            dma((16,)),
            dma((16,)),
            dma((16,)),
        ]

    def rows(self, start, count=1):
        return pl.ds(pl.multiple_of(start * self.part, self.part), count * self.part)

    def first(self):
        p = self.place
        theirs = self.rows((1 - p.core) * 16, 16)
        return remote(self.pay.at[:, theirs, :], self.half, self.s1.at[0], self.r1.at[0], p.partner)

    def second(self, k):
        device, there = self.place.xy_peer(k)
        return remote(self.whole.at[:, self.rows(there), :], self.got.at[k], self.s2.at[k], self.r2.at[k], device)

    def third(self, k):
        p = self.place
        return remote(self.along.at[p.zz], self.along.at[p.zz], self.s3.at[k], self.r3.at[k], p.z_peer(k))

    def spot(self, row):
        rows = self.rows(self.place.core * 16 + row)
        return self.out.at[:, :, rows, :] if self.both else self.out.at[:, rows, :]

    def fourth(self, k, row):
        spot = self.spot(row)
        return remote(spot, spot, self.s4.at[k], self.r4.at[k], self.place.xy_peer(k)[0])

    def fifth(self, k, row):
        spot = self.spot(row)
        return remote(spot, spot, self.s5.at[k], self.r5.at[k], self.place.partner)

    def part1(self):
        self.first().start()

    def part2(self):
        self.first().wait()
        mine = self.rows(self.place.core * 16, 16)
        both = self.pay[:, mine, :].astype(F32) + self.half[...].astype(F32)
        self.whole[...] = both.astype(self.whole.dtype)
        for k in range(1, 16):
            self.second(k).start()

    def part3(self):
        p = self.place
        for k in range(1, 16):
            self.second(k).wait()
        total = self.whole[:, self.rows(p.here), :].astype(F32)
        for k in range(1, 16):
            total = total + self.got[k].astype(F32)
        self.along[p.zz] = total.astype(self.along.dtype)
        for k in range(1, 8):
            self.third(k).start()

    def part4(self):
        p = self.place
        for k in range(1, 8):
            self.third(k).wait()
        along = [self.along[i].astype(F32) for i in range(8)]
        lower = along[0] + along[1] + along[2] + along[3]
        upper = along[4] + along[5] + along[6] + along[7]
        rows = self.rows(p.core * 16 + p.here)
        if self.both:
            self.out[0, :, rows, :] = lower
            self.out[1, :, rows, :] = upper
        else:
            self.out[:, rows, :] = lower + upper
        for k in range(1, 16):
            self.fourth(k, p.here).start()
        self.fifth(0, p.here).start()

    def part5(self):
        p = self.place
        for k in range(1, 16):
            source = p.xy_source(k)
            self.fourth(k, source).wait_recv()
            self.fifth(k, source).start()

    def end(self):
        p = self.place
        for k in range(1, 16):
            self.fourth(k, p.here).wait_send()
        for k in range(16):
            self.fifth(k, p.here).wait()


def invert_block(block):
    lane = lax.broadcasted_iota(jnp.int32, (8, 128), 1)
    sub = lax.broadcasted_iota(jnp.int32, (8, 128), 0)
    rows = [block[8 * p : 8 * p + 8] for p in range(16)]
    for p in range(16):
        k = 8 * p
        panel = rows[p]
        d = [[jnp.broadcast_to(panel[i : i + 1, k + j : k + j + 1], (8, 128)) for j in range(i + 1)] for i in range(8)]
        inside = (lane >= k) & (lane < k + 8)
        start = jnp.where(inside, (lane == k + sub).astype(F32), panel)
        acc = [jnp.broadcast_to(start[s : s + 1, :], (8, 128)) for s in range(8)]
        done = []
        for j in range(8):
            r = lax.rsqrt(d[j][j])
            xj = acc[j] * r
            done.append(xj)
            low = [None] * 8
            for i in range(j + 1, 8):
                low[i] = d[i][j] * r
            for i in range(j + 1, 8):
                for m in range(j + 1, i + 1):
                    d[i][m] = d[i][m] - low[i] * low[m]
                acc[i] = acc[i] - low[i] * xj
        x = done[0]
        for s in range(1, 8):
            x = jnp.where(sub == s, done[s], x)
        rows[p] = x
        if p < 15:
            ahead = jnp.where(inside, 0.0, rows[p + 1])
            pick = lane == k + 8 + sub
            for r in range(8):
                ahead = ahead - jnp.sum(jnp.where(pick, done[r], 0.0), axis=1, keepdims=True) * done[r]
            rows[p + 1] = ahead
        if p < 14:
            right = jnp.where(lane >= k + 16, x, 0.0)
            update = fdot(right, x, TN)
            for q in range(p + 2, 16):
                rows[q] = jnp.where(inside, 0.0, rows[q]) - update[8 * q : 8 * q + 8]
    whole = jnp.concatenate(rows, axis=0)
    rr = lax.broadcasted_iota(jnp.int32, (128, 128), 0)
    cc = lax.broadcasted_iota(jnp.int32, (128, 128), 1)
    return jnp.where(cc <= rr, whole, 0.0)


def eliminate_step(c, offset, j):
    blocks = c.shape[0] // 128
    rr = lax.broadcasted_iota(jnp.int32, (128, 128), 0)
    cc = lax.broadcasted_iota(jnp.int32, (128, 128), 1)
    rows, cols = slice(128 * j, 128 * j + 128), slice(offset + 128 * j, offset + 128 * j + 128)
    inverse = invert_block(c[rows, cols])
    c[rows, cols] = (rr == cc).astype(F32)
    c[rows, :] = fdot(inverse, c[rows, :])
    for i in range(j + 1, blocks):
        below = slice(128 * i, 128 * i + 128)
        across = slice(offset + 128 * i, offset + 128 * i + 128)
        factor = c[rows, across]
        c[below, cols] = jnp.zeros((128, 128), F32)
        c[below, :] = c[below, :] - fdot(factor, c[rows, :], TN)


def clear_right(c, offset):
    for i in range(c.shape[0] // 128):
        for j in range(i + 1, c.shape[0] // 128):
            c[128 * i : 128 * i + 128, offset + 128 * j : offset + 128 * j + 128] = jnp.zeros((128, 128), F32)


def spread(c, slabs, tiles, offset):
    for t, (r, col) in enumerate(tiles):
        for h in range(2):
            lo = offset + 256 * col + 128 * h
            c[256 * r : 256 * r + 256, lo : lo + 128] = slabs(2 * t + h)


def first_factor_kernel(
    orb, orb_far, pot, s_sum, w, h_pay, half, edge, keep, recv, edge_recv, *scratch
):
    place = Place()
    s_pay = scratch[23]
    total = Sum(place, True, s_pay, s_sum, scratch[:14])
    sems = scratch[14:16]
    xlo, xhi, ylo, yhi, hpsi, send, edge_send = scratch[16:23]
    rows = lambda i: pl.ds(64 * i, 64)
    pieces = [(edge_send, edge_recv)] + [(send.at[rows(i), :], recv.at[rows(i), :]) for i in range(8)]
    swap = Bulk(pieces, place.opposite, sems, 0)
    quarters = [pl.ds(128 * i, 128) for i in range(4)]
    x_up = Bulk(
        [(orb_far.at[q, pl.ds(1024, 1024)], xlo.at[q, :]) for q in quarters], place.next_x, sems, 9
    )
    x_down = Bulk([(orb_far.at[q, pl.ds(0, 1024)], xhi.at[q, :]) for q in quarters], place.last_x, sems, 13)
    y_up = Bulk(
        [(orb_far.at[:, pl.ds(512 * a + 256, 256)], ylo.at[:, pl.ds(256 * a, 256)]) for a in range(4)],
        place.next_y,
        sems,
        17,
    )
    y_down = Bulk(
        [(orb_far.at[:, pl.ds(512 * a, 256)], yhi.at[:, pl.ds(256 * a, 256)]) for a in range(4)],
        place.last_y,
        sems,
        21,
    )
    place.greet(True)
    y_up.start()
    pack(place.band, orb, pot, s_pay, send, keep, edge_send)
    total.part1()
    total.part2()
    x_up.start()
    x_down.start()
    total.part3()
    y_down.start()
    edge_differences(place.band, orb, edge)
    total.part4()
    swap.start()
    x_up.wait()
    x_down.wait()
    total.part5()
    y_up.wait()
    y_down.wait()
    hamiltonian(place.band, orb, xlo, xhi, ylo, yhi, pot, hpsi, half)
    for t, (r, c) in enumerate(TILES_LOW):
        tile = bdot(hpsi[256 * r : 256 * r + 256, :], orb[256 * c : 256 * c + 256, :], NT)
        store_tall(h_pay, t, tile)
    total.end()
    w[256:512, 0:256] = jnp.zeros((256, 256), F32)
    spread(w, lambda i: s_sum[0, i], TILES_UP, 0)
    for j in range(4):
        eliminate_step(w, 0, j)
    clear_right(w, 0)
    swap.wait()


def second_factor_kernel(
    s, h_pay, half, edge, keep, keep_far, recv, edge_recv, w0, c, own_sum, cross_sum, rest, *scratch
):
    place = Place()
    x_pay, x_sum, cross_pay, cross_s = scratch[42:46]
    over = Sum(place, False, x_pay, x_sum, scratch[:14])
    own = Sum(place, True, h_pay, own_sum, scratch[14:28])
    cross = Sum(place, False, cross_pay, cross_sum, scratch[28:42])
    sems = scratch[46:48]
    rows = lambda i: pl.ds(64 * i, 64)
    pieces = [(keep_far.at[rows(i), :], rest.at[rows(i), :]) for i in range(8)]
    tail = Bulk(pieces, place.opposite, sems, 0, place.band == 0, place.band == 1)
    place.greet(False)
    own.part1()
    tail.start(2)
    cross_products(place.band, keep, recv, x_pay)
    over.part1()
    cross_products(place.band, half, recv, cross_pay, edge, edge_recv)
    over.part2()
    cross.part1()
    own.part2()
    over.part3()
    tail.start(2)
    over.part4()
    cross.part2()
    own.part3()
    tail.start(2)
    over.part5()
    own.part4()
    over.end()
    for t, (r, col) in enumerate(TILES_ALL):
        for h in range(2):
            lo = 256 * col + 128 * h
            cross_s[256 * r : 256 * r + 256, lo : lo + 128] = x_sum[2 * t + h]
    first = split(w0[...])
    low = split(dot3(split(cross_s[...]), first, NT))
    c[256:512, 512:768] = jnp.zeros((256, 256), F32)
    spread(c, lambda i: s[1, i], TILES_UP, 512)
    c[:, 512:1024] = c[:, 512:1024] - dot3(low, low, NT)
    c[:, 0:512] = -dot3(low, first)
    cross.part3()
    tail.start()
    eliminate_step(c, 512, 0)
    own.part5()
    cross.part4()
    eliminate_step(c, 512, 1)
    eliminate_step(c, 512, 2)
    cross.part5()
    eliminate_step(c, 512, 3)
    clear_right(c, 512)
    own.end()
    cross.end()
    tail.wait()


def split(a):
    high = a.astype(BF16)
    return high, (a - high.astype(F32)).astype(BF16)


def dot3(a, b, dims=NN):
    return bdot(a[0], b[0], dims) + (bdot(a[0], b[1], dims) + bdot(a[1], b[0], dims))


def last_kernel(
    s, hown, cross, w0, c, recv_far, rest_far, own_far, h_sub, rotated, rot_other, rot_own, wh, wl, mh, ml, *scratch
):
    band = lax.axis_index("band")
    recv, rest, own, out, sems = scratch
    loads = [
        pltpu.make_async_copy(far, near, sems.at[i])
        for i, (far, near) in enumerate(((recv_far, recv), (rest_far, rest), (own_far, own)))
    ]
    for load in loads:
        load.start()

    @pl.when(band == 0)
    def _():
        rot_own[...] = w0[...].astype(BF16)
        rot_other[...] = jnp.zeros((512, 512), BF16)

    @pl.when(band == 1)
    def _():
        rot_own[...] = c[:, 512:1024].astype(BF16)
        rot_other[...] = c[:, 0:512].astype(BF16)

    for load in loads:
        load.wait()
    rotate(band, rot_other, rot_own, recv, rest, own, out)
    store = pltpu.make_async_copy(out, rotated, sems.at[3])
    store.start()

    for r in range(4):
        source = w0 if r < 2 else c
        base = 256 * (r % 2)
        width = 512 if r < 2 else 1024
        high, lowpart = split(source[base : base + 256, :])
        wh[256 * r : 256 * r + 256, 0:width] = high
        wl[256 * r : 256 * r + 256, 0:width] = lowpart

    rr = lax.broadcasted_iota(jnp.int32, (256, 256), 0)
    cc = lax.broadcasted_iota(jnp.int32, (256, 256), 1)
    weight = jnp.where(cc < rr, 1.0, jnp.where(cc == rr, 0.5, 0.0)).astype(F32)

    def wide(tall):
        return jnp.concatenate([tall[0:256, :], tall[256:512, :]], axis=1)

    half = {}
    for b in range(2):
        for t, (r, col) in enumerate(TILES_LOW):
            tile = wide(hown[b, t])
            if r == col:
                tile = tile * weight
            half[2 * b + r, 2 * b + col] = split(tile)
    for t, (r, col) in enumerate(TILES_ALL):
        half[2 + r, col] = split(wide(cross[t]))

    def block(high, lowpart, r, col):
        rows, cols = slice(256 * r, 256 * r + 256), slice(256 * col, 256 * col + 256)
        return high[rows, cols], lowpart[rows, cols]

    for r in range(4):
        for col in range(r + 1):
            total = None
            for k in range(col, r + 1):
                part = dot3(block(wh, wl, r, k), half[k, col])
                total = part if total is None else total + part
            high, lowpart = split(total)
            mh[256 * r : 256 * r + 256, 256 * col : 256 * col + 256] = high
            ml[256 * r : 256 * r + 256, 256 * col : 256 * col + 256] = lowpart

    vmean = jnp.sum(s[0, 0, 128:136, :]) / (128 * CELLS)
    shift = jnp.where(rr == cc, vmean, 0.0)

    def product(r, col):
        total = None
        for k in range(min(r, col) + 1):
            part = dot3(block(mh, ml, r, k), block(wh, wl, col, k), NT)
            total = part if total is None else total + part
        return total

    for r in range(4):
        for col in range(r + 1):
            tile = product(r, col)
            if r == col:
                h_sub[256 * r : 256 * r + 256, 256 * r : 256 * r + 256] = tile + tile.T - shift
            else:
                tile = tile + product(col, r).T
                h_sub[256 * r : 256 * r + 256, 256 * col : 256 * col + 256] = tile
                h_sub[256 * col : 256 * col + 256, 256 * r : 256 * r + 256] = tile.T
    store.wait()


def circle_weights():
    row = lax.broadcasted_iota(jnp.int32, (128, 128), 0)
    col = lax.broadcasted_iota(jnp.int32, (128, 128), 1)
    return row, col, step_weights((row - col + 128) % 128)


def step_weights(away):
    near = (away == 1) | (away == 127)
    far = (away == 2) | (away == 126)
    return jnp.where(near, 16.0, jnp.where(far, -1.0, 0.0))


def edge_differences(band, orb, edge):
    row, _, _ = circle_weights()
    _, owner, level = edge_cells()
    weights = jnp.where(row < 64, step_weights((row - level + 128) % 128), 0.0)

    @pl.loop(0, 4)
    def _(step):
        rows = pl.ds(pl.multiple_of(step * 128, 128), 128)
        total = jnp.zeros((128, 128), F32)
        for i in range(16):
            total = total + bdot(orb[rows, 128 * i : 128 * i + 128], jnp.where(owner == i, weights, 0.0).astype(BF16))
        edge[rows, :] = jnp.where(band == 1, total * (-0.5 / 12.0), 0.0).astype(BF16)


def hamiltonian(band, orb, xlo, xhi, ylo, yhi, pot, hpsi, half):
    row, col, weights = circle_weights()
    full = jnp.where(row == col, -90.0, weights)
    outer = jnp.where((band == 0) & (row < 64) & (col >= 64), weights, 0.0)
    circles = jnp.concatenate([full, outer], axis=1).astype(BF16)
    pack = jnp.concatenate(packers(64 - 64 * band), axis=0)
    n = 32

    @pl.loop(0, HALF // n, unroll=2)
    def _(step):
        rows = pl.ds(pl.multiple_of(step * n, n), n)

        def slab(ref, i):
            return ref[rows, 128 * i : 128 * i + 128]

        def cell(a, b):
            if a < 0:
                return slab(xlo, (a + 2) * 4 + b)
            if a > 3:
                return slab(xhi, (a - 4) * 4 + b)
            if b < 0:
                return slab(ylo, a * 2 + b + 2)
            if b > 3:
                return slab(yhi, a * 2 + b - 4)
            return slab(orb, a * 4 + b)

        cells = jnp.concatenate([cell(i // 4, i % 4) for i in range(16)], axis=0)
        along = bdot(cells, circles)
        parts = [[], []]
        for i in range(16):
            a, b = i // 4, i % 4
            field = lambda i, j: cell(i, j).astype(F32)
            near = (field(a - 1, b) + field(a + 1, b)) + (field(a, b - 1) + field(a, b + 1))
            far = (field(a - 2, b) + field(a + 2, b)) + (field(a, b - 2) + field(a, b + 2))
            here = slice(n * i, n * i + n)
            value = (16.0 * near - far + along[here, :128]) * (-0.5 / 12.0) + pot[i : i + 1, :] * field(a, b)
            hpsi[rows, 128 * i : 128 * i + 128] = value.astype(BF16)
            parts[i % 2].append((value + along[here, 128:] * (0.5 / 12.0)).astype(BF16))
        sides = [jnp.concatenate(part, axis=0) for part in parts]
        packed = bdot(jnp.concatenate(sides, axis=1), pack)
        for m in range(8):
            half[rows, 128 * m : 128 * m + 128] = packed[n * m : n * m + n].astype(BF16)


def store_tall(out, t, tile):
    out[t, 0:256, :] = tile[:, :128].astype(out.dtype)
    out[t, 256:512, :] = tile[:, 128:].astype(out.dtype)


def cross_products(band, half, recv, out, edge=None, edge_recv=None):
    def products(left, right, corner):
        for t, (r, c) in enumerate(TILES_ALL):
            up, across = slice(256 * r, 256 * r + 256), slice(256 * c, 256 * c + 256)
            tile = bdot(left[up, 0:1024], right[across, 0:1024], NT)
            if corner:
                lane = lax.broadcasted_iota(jnp.int32, (256, 128), 1)
                corner_part = jnp.where(lane // 64 == c, edge[up, :].astype(F32), 0.0).astype(BF16)
                tile = tile + bdot(corner_part, edge_recv[...], NT)
            if edge is None:
                out[2 * t] = tile[:, :128]
                out[2 * t + 1] = tile[:, 128:]
            else:
                store_tall(out, t, tile)

    @pl.when(band == 1)
    def _():
        products(half, recv, edge is not None)

    @pl.when(band == 0)
    def _():
        products(recv, half, False)


def rotate(band, rot_other, rot_own, recv, rest, own, out):
    @pl.when(band == 0)
    def _():
        for i in range(4):
            there = slice(512 * i, 512 * i + 512)
            out[:, there] = bdot(rot_own[...], own[:, there]).astype(BF16)

    @pl.when(band == 1)
    def _():
        low_even, low_odd = packers(0)
        high_even, high_odd = packers(64)
        for m in range(8):
            cols = slice(128 * m, 128 * m + 128)
            low, high = recv[:, cols], rest[:, cols]
            even = (bdot(low, low_even, NT) + bdot(high, high_even, NT)).astype(BF16)
            odd = (bdot(low, low_odd, NT) + bdot(high, high_odd, NT)).astype(BF16)
            other = jnp.concatenate([even, odd], axis=1)
            there = slice(256 * m, 256 * m + 256)
            total = bdot(rot_own[...], own[:, there]) + bdot(rot_other[...], other)
            out[:, there] = total.astype(BF16)


def shards(orbitals, potential):
    orb = orbitals.reshape(HALF, CELLS)
    pot = potential.reshape(16, 128)
    slab = lambda n: jax.ShapeDtypeStruct((n, 256, 128), F32)
    square = lambda n, t: jax.ShapeDtypeStruct((n, n), t)
    wide = lambda n: jax.ShapeDtypeStruct((HALF, n), BF16)
    tall = lambda n, t, *lead: jax.ShapeDtypeStruct(lead + (n, 512, 128), t)
    two = lambda n: jax.ShapeDtypeStruct((2, n, 256, 128), F32)
    dma = pltpu.SemaphoreType.DMA
    corner = jax.ShapeDtypeStruct((256, 128), BF16)
    s_sum, w0, h_pay, half, edge, keep, recv, edge_recv = call(
        first_factor_kernel,
        [two(6), square(512, F32), tall(3, F32), wide(1024), wide(128), wide(1024), wide(1024), corner],
        (orb, orb, pot),
        "first_factor",
        scratch=Sum.scratch(6)
        + [dma((25,)), dma((25,))]
        + [pltpu.VMEM((HALF, n), BF16) for n in (1024, 1024, 1024, 1024, CELLS, 1024)]
        + [pltpu.VMEM((256, 128), BF16), pltpu.VMEM((6, 256, 128), F32)],
        collective=0,
        far_in=(1,),
        far_out=(6, 7),
    )
    c, h_sum, hx_sum, rest = call(
        second_factor_kernel,
        [jax.ShapeDtypeStruct((HALF, 1024), F32), tall(3, F32, 2), tall(4, F32), wide(1024)],
        (s_sum, h_pay, half, edge, keep, keep, recv, edge_recv, w0),
        "second_factor",
        scratch=Sum.scratch(8)
        + Sum.scratch(3, 512)
        + Sum.scratch(4, 512)
        + [pltpu.VMEM((8, 256, 128), F32)] * 2
        + [pltpu.VMEM((4, 512, 128), F32), pltpu.VMEM((512, 512), F32)]
        + [dma((8,)), dma((8,))],
        collective=1,
        far_in=(5,),
        far_out=(3,),
    )
    h_sub, rotated = call(
        last_kernel,
        [square(1024, F32), wide(CELLS)],
        (s_sum, h_sum, hx_sum, w0, c, recv, rest, orb),
        "subspace_matrix",
        scratch=[pltpu.VMEM((HALF, HALF), BF16)] * 2
        + [pltpu.VMEM((1024, 1024), BF16)] * 4
        + [pltpu.VMEM((HALF, n), BF16) for n in (1024, 1024, CELLS, CELLS)]
        + [dma((4,))],
        far_in=(5, 6, 7),
        far_out=(1,),
    )
    return rotated.reshape(orbitals.shape), h_sub


def solution(mesh):
    in_specs = (P("band", "domain", None), P("domain", None))
    out_specs = (P("band", "domain", None), P())
    return jax.shard_map(shards, mesh=mesh, in_specs=in_specs, out_specs=out_specs, check_vma=False)
```

```python
import jax
import jax.numpy as jnp
from jax import lax
from jax.experimental import pallas as pl
from jax.experimental.pallas import tpu as pltpu
from jax.sharding import PartitionSpec as P

MESH = pl.DeviceIdType.MESH
HI = lax.Precision.HIGHEST
NN = (((1,), (0,)), ((), ()))
NT = (((1,), (1,)), ((), ()))
TN = (((0,), (0,)), ((), ()))
F32 = jnp.float32
BF16 = jnp.bfloat16
VMEM = pl.BlockSpec(memory_space=pltpu.VMEM)
ANY = pl.BlockSpec(memory_space=pl.ANY)
MIB = 2**20
CELLS = 2048
HALF = 512
TILES_UP = ((0, 0), (0, 1), (1, 1))
TILES_LOW = ((0, 0), (1, 0), (1, 1))
TILES_ALL = ((0, 0), (0, 1), (1, 0), (1, 1))


def fdot(a, b, dims=NN):
    return lax.dot_general(a, b, dims, precision=HI, preferred_element_type=F32)


def bdot(a, b, dims=NN):
    return lax.dot_general(a, b, dims, preferred_element_type=F32)


def call(kernel, outs, args, name, scratch=(), collective=None, limit=48, flops=0, far_in=(), far_out=()):
    params = dict(vmem_limit_bytes=limit * MIB)
    if collective is not None:
        params.update(collective_id=collective, has_side_effects=True)
    return pl.pallas_call(
        kernel,
        out_shape=outs,
        in_specs=[ANY if i in far_in else VMEM for i in range(len(args))],
        out_specs=[ANY if i in far_out else VMEM for i in range(len(outs))],
        scratch_shapes=list(scratch),
        compiler_params=pltpu.CompilerParams(**params),
        cost_estimate=pl.CostEstimate(flops=flops, bytes_accessed=8 * MIB, transcendentals=0),
        name=name,
    )(*args)


def packers(lower):
    z = lax.broadcasted_iota(jnp.int32, (128, 128), 0)
    lane = lax.broadcasted_iota(jnp.int32, (128, 128), 1)
    even = (lane < 64) & (z == lane + lower)
    odd = (lane >= 64) & (z == lane - 64 + lower)
    return even.astype(F32).astype(BF16), odd.astype(F32).astype(BF16)


def edge_cells():
    lane = lax.broadcasted_iota(jnp.int32, (128, 128), 1)
    q = lane % 4
    return lane // 64, (lane % 64) // 4, jnp.where(q < 2, 64 + q, 124 + q)


def pack(band, orb, pot, pay, send, keep, edge_send):
    for t, (r, c) in enumerate(TILES_UP):
        tile = bdot(orb[256 * r : 256 * r + 256, :], orb[256 * c : 256 * c + 256, :], NT)
        pay[2 * t] = tile[:, :128]
        pay[2 * t + 1] = tile[:, 128:]
    pay[0, 128:136, :] = pot[0:8, :] + pot[8:16, :]
    z = lax.broadcasted_iota(jnp.int32, (128, 128), 0)
    side, owner, level = edge_cells()

    @pl.loop(0, 4)
    def _(step):
        rows = pl.ds(pl.multiple_of(step * 128, 128), 128)
        slab = lambda i: orb[rows, 128 * i : 128 * i + 128]
        for ref, lower in ((send, 64 * band), (keep, 64 - 64 * band)):
            even, odd = packers(lower)
            for m in range(8):
                packed = bdot(slab(2 * m), even) + bdot(slab(2 * m + 1), odd)
                ref[rows, 128 * m : 128 * m + 128] = packed.astype(BF16)

    @pl.loop(0, 2)
    def _(step):
        edge = jnp.zeros((128, 128), F32)
        for h in range(2):
            rows = pl.ds(pl.multiple_of(step * 128, 128) + 256 * h, 128)
            for i in range(16):
                pick = ((side == h) & (owner == i) & (z == level)).astype(F32).astype(BF16)
                edge = edge + bdot(orb[rows, 128 * i : 128 * i + 128], pick)
        edge_send[pl.ds(pl.multiple_of(step * 128, 128), 128), :] = edge.astype(BF16)


class Place:
    def __init__(self):
        self.band = lax.axis_index("band")
        dom = lax.axis_index("domain")
        self.x, self.y = dom // 32, (dom // 8) % 4
        self.z, self.core = (dom // 2) % 4, dom % 2
        self.here = self.x * 4 + self.y
        self.zz = self.band * 4 + self.z
        self.partner = self.at(self.band, self.x, self.y, self.z, 1 - self.core)
        self.opposite = (1 - self.band, dom)
        self.next_x = (self.band, (dom + 8) % 128)
        self.last_x = (self.band, (dom + 120) % 128)
        self.next_y = (self.band, (dom // 8) * 8 + (dom + 1) % 8)
        self.last_y = (self.band, (dom // 8) * 8 + (dom + 7) % 8)

    @staticmethod
    def at(b, xx, yy, zl, cc):
        return (b, ((xx * 4 + yy) * 4 + zl) * 2 + cc)

    def xy_peer(self, k):
        xx, yy = (self.x + k // 4) % 4, (self.y + k % 4) % 4
        return self.at(self.band, xx, yy, self.z, self.core), xx * 4 + yy

    def xy_source(self, k):
        return ((self.x + 4 - k // 4) % 4) * 4 + (self.y + 4 - k % 4) % 4

    def z_peer(self, k):
        other = (self.zz + k) % 8
        return self.at(other // 4, self.x, self.y, other % 4, self.core)

    def greet(self, y_too):
        barrier = pltpu.get_barrier_semaphore()
        peers = [self.partner]
        peers += [self.xy_peer(k)[0] for k in range(1, 16)]
        peers += [self.z_peer(k) for k in range(1, 8)]
        if y_too:
            band, dom = self.next_y
            peers.append((band, jnp.where(self.core == 0, self.last_y[1], dom)))
        for peer in peers:
            pl.semaphore_signal(barrier, inc=1, device_id=peer, device_id_type=MESH)
        pl.semaphore_wait(barrier, len(peers))


def remote(src, dst, send, recv, device):
    return pltpu.make_async_remote_copy(
        src_ref=src, dst_ref=dst, send_sem=send, recv_sem=recv, device_id=device, device_id_type=MESH
    )


class Bulk:
    def __init__(self, pieces, device, sems, first, condition=None, other=None):
        self.sems, self.first, self.device = sems, first, device
        self.pieces, self.condition, self.other = pieces, condition, other
        self.started = 0

    def copy(self, i):
        src, dst = self.pieces[i]
        return remote(src, dst, self.sems[0].at[self.first + i], self.sems[1].at[self.first + i], self.device)

    def start(self, count=None):
        stop = len(self.pieces) if count is None else self.started + count

        def body():
            for i in range(self.started, stop):
                self.copy(i).start()

        if self.condition is None:
            body()
        else:
            pl.when(self.condition)(body)
        self.started = stop

    def wait(self):
        if self.condition is None:
            for i in range(len(self.pieces)):
                self.copy(i).wait()
            return

        @pl.when(self.condition)
        def _():
            for i in range(len(self.pieces)):
                self.copy(i).wait_send()

        @pl.when(self.other)
        def _():
            for i in range(len(self.pieces)):
                self.copy(i).wait_recv()


class Sum:
    scratch_count = 4 + 10

    def __init__(self, place, both, pay, out, scratch):
        self.place, self.both, self.pay, self.out = place, both, pay, out
        self.part = (out.shape[-2] if pay is None else pay.shape[1]) // 32
        self.half, self.whole, self.got, self.along = scratch[:4]
        self.s1, self.r1, self.s2, self.r2, self.s3, self.r3, self.s4, self.r4, self.s5, self.r5 = scratch[4:14]

    @staticmethod
    def scratch(n, height=256, wire=F32):
        dma = pltpu.SemaphoreType.DMA
        return [
            pltpu.VMEM((n, height // 2, 128), wire),
            pltpu.VMEM((n, height // 2, 128), wire),
            pltpu.VMEM((16, n, height // 32, 128), wire),
            pltpu.VMEM((8, n, height // 32, 128), wire),
            dma((1,)),
            dma((1,)),
            dma((16,)),
            dma((16,)),
            dma((8,)),
            dma((8,)),
            dma((16,)),
            dma((16,)),
            dma((16,)),
            dma((16,)),
        ]

    def rows(self, start, count=1):
        return pl.ds(pl.multiple_of(start * self.part, self.part), count * self.part)

    def first(self):
        p = self.place
        theirs = self.rows((1 - p.core) * 16, 16)
        return remote(self.pay.at[:, theirs, :], self.half, self.s1.at[0], self.r1.at[0], p.partner)

    def second(self, k):
        device, there = self.place.xy_peer(k)
        return remote(self.whole.at[:, self.rows(there), :], self.got.at[k], self.s2.at[k], self.r2.at[k], device)

    def third(self, k):
        p = self.place
        return remote(self.along.at[p.zz], self.along.at[p.zz], self.s3.at[k], self.r3.at[k], p.z_peer(k))

    def spot(self, row):
        rows = self.rows(self.place.core * 16 + row)
        return self.out.at[:, :, rows, :] if self.both else self.out.at[:, rows, :]

    def fourth(self, k, row):
        spot = self.spot(row)
        return remote(spot, spot, self.s4.at[k], self.r4.at[k], self.place.xy_peer(k)[0])

    def fifth(self, k, row):
        spot = self.spot(row)
        return remote(spot, spot, self.s5.at[k], self.r5.at[k], self.place.partner)

    def part1(self):
        self.first().start()

    def part2(self):
        self.first().wait()
        mine = self.rows(self.place.core * 16, 16)
        both = self.pay[:, mine, :].astype(F32) + self.half[...].astype(F32)
        self.whole[...] = both.astype(self.whole.dtype)
        for k in range(1, 16):
            self.second(k).start()

    def partial(self):
        for k in range(1, 16):
            self.second(k).wait()
        total = self.whole[:, self.rows(self.place.here), :]
        for k in range(1, 16):
            total = total + self.got[k]
        return total

    def part3(self, total=None):
        self.along[self.place.zz] = self.partial() if total is None else total
        for k in range(1, 8):
            self.third(k).start()

    def part4(self):
        p = self.place
        for k in range(1, 8):
            self.third(k).wait()
        along = [self.along[i].astype(F32) for i in range(8)]
        lower = along[0] + along[1] + along[2] + along[3]
        upper = along[4] + along[5] + along[6] + along[7]
        rows = self.rows(p.core * 16 + p.here)
        if self.both:
            self.out[0, :, rows, :] = lower
            self.out[1, :, rows, :] = upper
        else:
            self.out[:, rows, :] = lower + upper
        for k in range(1, 16):
            self.fourth(k, p.here).start()
        self.fifth(0, p.here).start()

    def part5(self):
        p = self.place
        for k in range(1, 16):
            source = p.xy_source(k)
            self.fourth(k, source).wait_recv()
            self.fifth(k, source).start()

    def end(self):
        p = self.place
        for k in range(1, 16):
            self.fourth(k, p.here).wait_send()
        for k in range(16):
            self.fifth(k, p.here).wait()


def invert_block(block):
    lane = lax.broadcasted_iota(jnp.int32, (8, 128), 1)
    sub = lax.broadcasted_iota(jnp.int32, (8, 128), 0)
    rows = [block[8 * p : 8 * p + 8] for p in range(16)]
    for p in range(16):
        k = 8 * p
        panel = rows[p]
        d = [[jnp.broadcast_to(panel[i : i + 1, k + j : k + j + 1], (8, 128)) for j in range(i + 1)] for i in range(8)]
        inside = (lane >= k) & (lane < k + 8)
        start = jnp.where(inside, (lane == k + sub).astype(F32), panel)
        acc = [jnp.broadcast_to(start[s : s + 1, :], (8, 128)) for s in range(8)]
        done = []
        for j in range(8):
            r = lax.rsqrt(d[j][j])
            xj = acc[j] * r
            done.append(xj)
            low = [None] * 8
            for i in range(j + 1, 8):
                low[i] = d[i][j] * r
            for i in range(j + 1, 8):
                for m in range(j + 1, i + 1):
                    d[i][m] = d[i][m] - low[i] * low[m]
                acc[i] = acc[i] - low[i] * xj
        x = done[0]
        for s in range(1, 8):
            x = jnp.where(sub == s, done[s], x)
        rows[p] = x
        if p < 15:
            ahead = jnp.where(inside, 0.0, rows[p + 1])
            pick = lane == k + 8 + sub
            for r in range(8):
                ahead = ahead - jnp.sum(jnp.where(pick, done[r], 0.0), axis=1, keepdims=True) * done[r]
            rows[p + 1] = ahead
        if p < 14:
            right = jnp.where(lane >= k + 16, x, 0.0)
            update = fdot(right, x, TN)
            for q in range(p + 2, 16):
                rows[q] = jnp.where(inside, 0.0, rows[q]) - update[8 * q : 8 * q + 8]
    whole = jnp.concatenate(rows, axis=0)
    rr = lax.broadcasted_iota(jnp.int32, (128, 128), 0)
    cc = lax.broadcasted_iota(jnp.int32, (128, 128), 1)
    return jnp.where(cc <= rr, whole, 0.0)


def eliminate_step(c, offset, j, between=None):
    blocks = c.shape[0] // 128
    rr = lax.broadcasted_iota(jnp.int32, (128, 128), 0)
    cc = lax.broadcasted_iota(jnp.int32, (128, 128), 1)
    rows, cols = slice(128 * j, 128 * j + 128), slice(offset + 128 * j, offset + 128 * j + 128)
    inverse = invert_block(c[rows, cols])
    c[rows, cols] = (rr == cc).astype(F32)
    c[rows, :] = fdot(inverse, c[rows, :])
    if between is not None:
        between()
    for i in range(j + 1, blocks):
        below = slice(128 * i, 128 * i + 128)
        across = slice(offset + 128 * i, offset + 128 * i + 128)
        factor = c[rows, across]
        c[below, cols] = jnp.zeros((128, 128), F32)
        c[below, :] = c[below, :] - fdot(factor, c[rows, :], TN)


def clear_right(c, offset):
    for i in range(c.shape[0] // 128):
        for j in range(i + 1, c.shape[0] // 128):
            c[128 * i : 128 * i + 128, offset + 128 * j : offset + 128 * j + 128] = jnp.zeros((128, 128), F32)


def spread(c, slabs, tiles, offset):
    for t, (r, col) in enumerate(tiles):
        for h in range(2):
            lo = offset + 256 * col + 128 * h
            c[256 * r : 256 * r + 256, lo : lo + 128] = slabs(2 * t + h)


def first_factor_kernel(
    orb, orb_far, pot, s_sum, w, h_part, half, edge, keep, recv, edge_recv, *scratch
):
    place = Place()
    s_pay, h_pay = scratch[23:25]
    own = Sum(place, True, h_pay, None, scratch[25:39])
    total = Sum(place, True, s_pay, s_sum, scratch[:14])
    sems = scratch[14:16]
    xlo, xhi, ylo, yhi, hpsi, send, edge_send = scratch[16:23]
    rows = lambda i: pl.ds(32 * i, 32)
    pieces = [(edge_send, edge_recv)] + [(send.at[rows(i), :], recv.at[rows(i), :]) for i in range(16)]
    swap = Bulk(pieces, place.opposite, sems, 0)
    quarters = [pl.ds(128 * i, 128) for i in range(4)]
    x_up = Bulk(
        [(orb_far.at[q, pl.ds(1024, 1024)], xlo.at[q, :]) for q in quarters], place.next_x, sems, 17
    )
    x_down = Bulk([(orb_far.at[q, pl.ds(0, 1024)], xhi.at[q, :]) for q in quarters], place.last_x, sems, 21)
    y_up = Bulk(
        [(orb_far.at[:, pl.ds(512 * a + 256, 256)], ylo.at[:, pl.ds(256 * a, 256)]) for a in range(4)],
        place.next_y,
        sems,
        25,
    )
    y_down = Bulk(
        [(orb_far.at[:, pl.ds(512 * a, 256)], yhi.at[:, pl.ds(256 * a, 256)]) for a in range(4)],
        place.last_y,
        sems,
        29,
    )
    place.greet(True)
    y_up.start()
    pack(place.band, orb, pot, s_pay, send, keep, edge_send)
    total.part1()
    total.part2()
    x_up.start()
    x_down.start()
    total.part3()
    y_down.start()
    edge_differences(place.band, orb, edge)
    total.part4()
    swap.start(6)
    total.part5()
    swap.start(3)
    x_up.wait()
    x_down.wait()
    y_up.wait()
    y_down.wait()
    swap.start(3)
    hamiltonian(place.band, orb, xlo, xhi, ylo, yhi, pot, hpsi, half)
    swap.start()
    for t, (r, c) in enumerate(TILES_LOW):
        tile = bdot(hpsi[256 * r : 256 * r + 256, :], orb[256 * c : 256 * c + 256, :], NT)
        store_tall(h_pay, t, tile)
    own.part1()
    total.end()
    w[256:512, 0:256] = jnp.zeros((256, 256), F32)
    spread(w, lambda i: s_sum[0, i], TILES_UP, 0)
    eliminate_step(w, 0, 0)
    own.part2()
    for j in range(1, 4):
        eliminate_step(w, 0, j)
    clear_right(w, 0)
    h_part[...] = own.partial()
    swap.wait()


def second_factor_kernel(
    s, h_part, half, edge, keep, keep_far, recv, edge_recv, w0, c, own_sum, cross_sum, rest, *scratch
):
    place = Place()
    x_pay, x_sum, cross_pay, cross_s = scratch[42:46]
    over = Sum(place, False, x_pay, x_sum, scratch[:14])
    own = Sum(place, True, None, own_sum, scratch[14:28])
    cross = Sum(place, False, cross_pay, cross_sum, scratch[28:42])
    sems = scratch[46:48]
    rows = lambda i: pl.ds(32 * i, 32)
    pieces = [(keep_far.at[rows(i), :], rest.at[rows(i), :]) for i in range(16)]
    tail = Bulk(pieces, place.opposite, sems, 0, place.band == 0, place.band == 1)
    place.greet(False)
    own.part3(h_part[...])
    tail.start(3)
    cross_products(place.band, keep, recv, x_pay)
    over.part1()
    cross_products(place.band, half, recv, cross_pay, edge, edge_recv)
    over.part2()
    cross.part1()
    over.part3()
    tail.start(1)
    over.part4()
    tail.start(2)
    cross.part2()
    own.part4()
    over.part5()
    tail.start(2)
    over.end()
    for t, (r, col) in enumerate(TILES_ALL):
        for h in range(2):
            lo = 256 * col + 128 * h
            cross_s[256 * r : 256 * r + 256, lo : lo + 128] = x_sum[2 * t + h]
    first = split(w0[...])
    low = split(dot3(split(cross_s[...]), first, NT))
    c[256:512, 512:768] = jnp.zeros((256, 256), F32)
    spread(c, lambda i: s[1, i], TILES_UP, 512)
    c[:, 512:1024] = c[:, 512:1024] - dot3(low, low, NT)
    c[:, 0:512] = -dot3(low, first)
    cross.part3()
    tail.start(1)
    own.part5()
    more = lambda: tail.start(1)
    eliminate_step(c, 512, 0, more)
    more()
    cross.part4()
    eliminate_step(c, 512, 1, more)
    more()
    eliminate_step(c, 512, 2, more)
    tail.start()
    cross.part5()
    eliminate_step(c, 512, 3)
    clear_right(c, 512)
    own.end()
    cross.end()
    tail.wait()


def split(a):
    high = a.astype(BF16)
    return high, (a - high.astype(F32)).astype(BF16)


def dot3(a, b, dims=NN):
    return bdot(a[0], b[0], dims) + (bdot(a[0], b[1], dims) + bdot(a[1], b[0], dims))


def last_kernel(
    s, hown, cross, w0, c, recv_far, rest_far, own_far, h_sub, rotated, rot_other, rot_own, wh, wl, mh, ml, *scratch
):
    band = lax.axis_index("band")
    recv, rest, own, out, sems = scratch
    loads = [
        pltpu.make_async_copy(far, near, sems.at[i])
        for i, (far, near) in enumerate(((recv_far, recv), (rest_far, rest), (own_far, own)))
    ]
    for load in loads:
        load.start()

    @pl.when(band == 0)
    def _():
        rot_own[...] = w0[...].astype(BF16)
        rot_other[...] = jnp.zeros((512, 512), BF16)

    @pl.when(band == 1)
    def _():
        rot_own[...] = c[:, 512:1024].astype(BF16)
        rot_other[...] = c[:, 0:512].astype(BF16)

    for load in loads:
        load.wait()
    rotate(band, rot_other, rot_own, recv, rest, own, out)
    store = pltpu.make_async_copy(out, rotated, sems.at[3])
    store.start()

    for r in range(4):
        source = w0 if r < 2 else c
        base = 256 * (r % 2)
        width = 512 if r < 2 else 1024
        high, lowpart = split(source[base : base + 256, :])
        wh[256 * r : 256 * r + 256, 0:width] = high
        wl[256 * r : 256 * r + 256, 0:width] = lowpart

    rr = lax.broadcasted_iota(jnp.int32, (256, 256), 0)
    cc = lax.broadcasted_iota(jnp.int32, (256, 256), 1)
    weight = jnp.where(cc < rr, 1.0, jnp.where(cc == rr, 0.5, 0.0)).astype(F32)

    def wide(tall):
        return jnp.concatenate([tall[0:256, :], tall[256:512, :]], axis=1)

    half = {}
    for b in range(2):
        for t, (r, col) in enumerate(TILES_LOW):
            tile = wide(hown[b, t])
            if r == col:
                tile = tile * weight
            half[2 * b + r, 2 * b + col] = split(tile)
    for t, (r, col) in enumerate(TILES_ALL):
        half[2 + r, col] = split(wide(cross[t]))

    def block(high, lowpart, r, col):
        rows, cols = slice(256 * r, 256 * r + 256), slice(256 * col, 256 * col + 256)
        return high[rows, cols], lowpart[rows, cols]

    for r in range(4):
        for col in range(r + 1):
            total = None
            for k in range(col, r + 1):
                part = dot3(block(wh, wl, r, k), half[k, col])
                total = part if total is None else total + part
            high, lowpart = split(total)
            mh[256 * r : 256 * r + 256, 256 * col : 256 * col + 256] = high
            ml[256 * r : 256 * r + 256, 256 * col : 256 * col + 256] = lowpart

    vmean = jnp.sum(s[0, 0, 128:136, :]) / (128 * CELLS)
    shift = jnp.where(rr == cc, vmean, 0.0)

    def product(r, col):
        total = None
        for k in range(min(r, col) + 1):
            part = dot3(block(mh, ml, r, k), block(wh, wl, col, k), NT)
            total = part if total is None else total + part
        return total

    for r in range(4):
        for col in range(r + 1):
            tile = product(r, col)
            if r == col:
                h_sub[256 * r : 256 * r + 256, 256 * r : 256 * r + 256] = tile + tile.T - shift
            else:
                tile = tile + product(col, r).T
                h_sub[256 * r : 256 * r + 256, 256 * col : 256 * col + 256] = tile
                h_sub[256 * col : 256 * col + 256, 256 * r : 256 * r + 256] = tile.T
    store.wait()


def circle_weights():
    row = lax.broadcasted_iota(jnp.int32, (128, 128), 0)
    col = lax.broadcasted_iota(jnp.int32, (128, 128), 1)
    return row, col, step_weights((row - col + 128) % 128)


def step_weights(away):
    near = (away == 1) | (away == 127)
    far = (away == 2) | (away == 126)
    return jnp.where(near, 16.0, jnp.where(far, -1.0, 0.0))


def edge_differences(band, orb, edge):
    row, _, _ = circle_weights()
    _, owner, level = edge_cells()
    weights = jnp.where(row < 64, step_weights((row - level + 128) % 128), 0.0)

    @pl.loop(0, 4)
    def _(step):
        rows = pl.ds(pl.multiple_of(step * 128, 128), 128)
        total = jnp.zeros((128, 128), F32)
        for i in range(16):
            total = total + bdot(orb[rows, 128 * i : 128 * i + 128], jnp.where(owner == i, weights, 0.0).astype(BF16))
        edge[rows, :] = jnp.where(band == 1, total * (-0.5 / 12.0), 0.0).astype(BF16)


def hamiltonian(band, orb, xlo, xhi, ylo, yhi, pot, hpsi, half):
    row, col, weights = circle_weights()
    full = jnp.where(row == col, -90.0, weights)
    outer = jnp.where((band == 0) & (row < 64) & (col >= 64), weights, 0.0)
    circles = jnp.concatenate([full, outer], axis=1).astype(BF16)
    pack = jnp.concatenate(packers(64 - 64 * band), axis=0)
    n = 32

    @pl.loop(0, HALF // n, unroll=2)
    def _(step):
        rows = pl.ds(pl.multiple_of(step * n, n), n)

        def slab(ref, i):
            return ref[rows, 128 * i : 128 * i + 128]

        def cell(a, b):
            if a < 0:
                return slab(xlo, (a + 2) * 4 + b)
            if a > 3:
                return slab(xhi, (a - 4) * 4 + b)
            if b < 0:
                return slab(ylo, a * 2 + b + 2)
            if b > 3:
                return slab(yhi, a * 2 + b - 4)
            return slab(orb, a * 4 + b)

        cells = jnp.concatenate([cell(i // 4, i % 4) for i in range(16)], axis=0)
        along = bdot(cells, circles)
        parts = [[], []]
        for i in range(16):
            a, b = i // 4, i % 4
            field = lambda i, j: cell(i, j).astype(F32)
            near = (field(a - 1, b) + field(a + 1, b)) + (field(a, b - 1) + field(a, b + 1))
            far = (field(a - 2, b) + field(a + 2, b)) + (field(a, b - 2) + field(a, b + 2))
            here = slice(n * i, n * i + n)
            value = (16.0 * near - far + along[here, :128]) * (-0.5 / 12.0) + pot[i : i + 1, :] * field(a, b)
            hpsi[rows, 128 * i : 128 * i + 128] = value.astype(BF16)
            parts[i % 2].append((value + along[here, 128:] * (0.5 / 12.0)).astype(BF16))
        sides = [jnp.concatenate(part, axis=0) for part in parts]
        packed = bdot(jnp.concatenate(sides, axis=1), pack)
        for m in range(8):
            half[rows, 128 * m : 128 * m + 128] = packed[n * m : n * m + n].astype(BF16)


def store_tall(out, t, tile):
    out[t, 0:256, :] = tile[:, :128].astype(out.dtype)
    out[t, 256:512, :] = tile[:, 128:].astype(out.dtype)


def cross_products(band, half, recv, out, edge=None, edge_recv=None):
    def products(left, right, corner):
        for t, (r, c) in enumerate(TILES_ALL):
            up, across = slice(256 * r, 256 * r + 256), slice(256 * c, 256 * c + 256)
            tile = bdot(left[up, 0:1024], right[across, 0:1024], NT)
            if corner:
                lane = lax.broadcasted_iota(jnp.int32, (256, 128), 1)
                corner_part = jnp.where(lane // 64 == c, edge[up, :].astype(F32), 0.0).astype(BF16)
                tile = tile + bdot(corner_part, edge_recv[...], NT)
            if edge is None:
                out[2 * t] = tile[:, :128]
                out[2 * t + 1] = tile[:, 128:]
            else:
                store_tall(out, t, tile)

    @pl.when(band == 1)
    def _():
        products(half, recv, edge is not None)

    @pl.when(band == 0)
    def _():
        products(recv, half, False)


def rotate(band, rot_other, rot_own, recv, rest, own, out):
    @pl.when(band == 0)
    def _():
        for i in range(4):
            there = slice(512 * i, 512 * i + 512)
            out[:, there] = bdot(rot_own[...], own[:, there]).astype(BF16)

    @pl.when(band == 1)
    def _():
        low_even, low_odd = packers(0)
        high_even, high_odd = packers(64)
        for m in range(8):
            cols = slice(128 * m, 128 * m + 128)
            low, high = recv[:, cols], rest[:, cols]
            even = (bdot(low, low_even, NT) + bdot(high, high_even, NT)).astype(BF16)
            odd = (bdot(low, low_odd, NT) + bdot(high, high_odd, NT)).astype(BF16)
            other = jnp.concatenate([even, odd], axis=1)
            there = slice(256 * m, 256 * m + 256)
            total = bdot(rot_own[...], own[:, there]) + bdot(rot_other[...], other)
            out[:, there] = total.astype(BF16)


def shards(orbitals, potential):
    orb = orbitals.reshape(HALF, CELLS)
    pot = potential.reshape(16, 128)
    slab = lambda n: jax.ShapeDtypeStruct((n, 256, 128), F32)
    square = lambda n, t: jax.ShapeDtypeStruct((n, n), t)
    wide = lambda n: jax.ShapeDtypeStruct((HALF, n), BF16)
    tall = lambda n, t, *lead: jax.ShapeDtypeStruct(lead + (n, 512, 128), t)
    two = lambda n: jax.ShapeDtypeStruct((2, n, 256, 128), F32)
    dma = pltpu.SemaphoreType.DMA
    part = jax.ShapeDtypeStruct((3, 16, 128), F32)
    corner = jax.ShapeDtypeStruct((256, 128), BF16)
    s_sum, w0, h_part, half, edge, keep, recv, edge_recv = call(
        first_factor_kernel,
        [two(6), square(512, F32), part, wide(1024), wide(128), wide(1024), wide(1024), corner],
        (orb, orb, pot),
        "first_factor",
        scratch=Sum.scratch(6)
        + [dma((33,)), dma((33,))]
        + [pltpu.VMEM((HALF, n), BF16) for n in (1024, 1024, 1024, 1024, CELLS, 1024)]
        + [pltpu.VMEM((256, 128), BF16), pltpu.VMEM((6, 256, 128), F32), pltpu.VMEM((3, 512, 128), F32)]
        + Sum.scratch(3, 512),
        collective=0,
        far_in=(1,),
        far_out=(6, 7),
    )
    c, h_sum, hx_sum, rest = call(
        second_factor_kernel,
        [jax.ShapeDtypeStruct((HALF, 1024), F32), tall(3, F32, 2), tall(4, F32), wide(1024)],
        (s_sum, h_part, half, edge, keep, keep, recv, edge_recv, w0),
        "second_factor",
        scratch=Sum.scratch(8)
        + Sum.scratch(3, 512)
        + Sum.scratch(4, 512)
        + [pltpu.VMEM((8, 256, 128), F32)] * 2
        + [pltpu.VMEM((4, 512, 128), F32), pltpu.VMEM((512, 512), F32)]
        + [dma((16,)), dma((16,))],
        collective=1,
        far_in=(5,),
        far_out=(3,),
    )
    h_sub, rotated = call(
        last_kernel,
        [square(1024, F32), wide(CELLS)],
        (s_sum, h_sum, hx_sum, w0, c, recv, rest, orb),
        "subspace_matrix",
        scratch=[pltpu.VMEM((HALF, HALF), BF16)] * 2
        + [pltpu.VMEM((1024, 1024), BF16)] * 4
        + [pltpu.VMEM((HALF, n), BF16) for n in (1024, 1024, CELLS, CELLS)]
        + [dma((4,))],
        far_in=(5, 6, 7),
        far_out=(1,),
    )
    return rotated.reshape(orbitals.shape), h_sub


def solution(mesh):
    in_specs = (P("band", "domain", None), P("domain", None))
    out_specs = (P("band", "domain", None), P())
    return jax.shard_map(shards, mesh=mesh, in_specs=in_specs, out_specs=out_specs, check_vma=False)
```

```python
import jax
import jax.numpy as jnp
from jax import lax
from jax.experimental import pallas as pl
from jax.experimental.pallas import tpu as pltpu
from jax.sharding import PartitionSpec as P

MESH = pl.DeviceIdType.MESH
HI = lax.Precision.HIGHEST
NN = (((1,), (0,)), ((), ()))
NT = (((1,), (1,)), ((), ()))
TN = (((0,), (0,)), ((), ()))
F32 = jnp.float32
BF16 = jnp.bfloat16
VMEM = pl.BlockSpec(memory_space=pltpu.VMEM)
ANY = pl.BlockSpec(memory_space=pl.ANY)
MIB = 2**20
CELLS = 2048
HALF = 512
TILES_UP = ((0, 0), (0, 1), (1, 1))
TILES_LOW = ((0, 0), (1, 0), (1, 1))
TILES_ALL = ((0, 0), (0, 1), (1, 0), (1, 1))


def fdot(a, b, dims=NN):
    return lax.dot_general(a, b, dims, precision=HI, preferred_element_type=F32)


def bdot(a, b, dims=NN):
    return lax.dot_general(a, b, dims, preferred_element_type=F32)


def call(kernel, outs, args, name, scratch=(), collective=None, limit=48, flops=0, far_in=(), far_out=()):
    params = dict(vmem_limit_bytes=limit * MIB)
    if collective is not None:
        params.update(collective_id=collective, has_side_effects=True)
    return pl.pallas_call(
        kernel,
        out_shape=outs,
        in_specs=[ANY if i in far_in else VMEM for i in range(len(args))],
        out_specs=[ANY if i in far_out else VMEM for i in range(len(outs))],
        scratch_shapes=list(scratch),
        compiler_params=pltpu.CompilerParams(**params),
        cost_estimate=pl.CostEstimate(flops=flops, bytes_accessed=8 * MIB, transcendentals=0),
        name=name,
    )(*args)


def packers(lower):
    z = lax.broadcasted_iota(jnp.int32, (128, 128), 0)
    lane = lax.broadcasted_iota(jnp.int32, (128, 128), 1)
    even = (lane < 64) & (z == lane + lower)
    odd = (lane >= 64) & (z == lane - 64 + lower)
    return even.astype(F32).astype(BF16), odd.astype(F32).astype(BF16)


def edge_cells():
    lane = lax.broadcasted_iota(jnp.int32, (128, 128), 1)
    q = lane % 4
    return lane // 64, (lane % 64) // 4, jnp.where(q < 2, 64 + q, 124 + q)


def pack(band, orb, pot, pay, send, keep, edge_send):
    for t, (r, c) in enumerate(TILES_UP):
        tile = bdot(orb[256 * r : 256 * r + 256, :], orb[256 * c : 256 * c + 256, :], NT)
        pay[2 * t] = tile[:, :128]
        pay[2 * t + 1] = tile[:, 128:]
    pay[0, 128:136, :] = pot[0:8, :] + pot[8:16, :]
    z = lax.broadcasted_iota(jnp.int32, (128, 128), 0)
    side, owner, level = edge_cells()

    @pl.loop(0, 4)
    def _(step):
        rows = pl.ds(pl.multiple_of(step * 128, 128), 128)
        slab = lambda i: orb[rows, 128 * i : 128 * i + 128]
        for ref, lower in ((send, 64 * band), (keep, 64 - 64 * band)):
            even, odd = packers(lower)
            for m in range(8):
                packed = bdot(slab(2 * m), even) + bdot(slab(2 * m + 1), odd)
                ref[rows, 128 * m : 128 * m + 128] = packed.astype(BF16)

    @pl.loop(0, 2)
    def _(step):
        edge = jnp.zeros((128, 128), F32)
        for h in range(2):
            rows = pl.ds(pl.multiple_of(step * 128, 128) + 256 * h, 128)
            for i in range(16):
                pick = ((side == h) & (owner == i) & (z == level)).astype(F32).astype(BF16)
                edge = edge + bdot(orb[rows, 128 * i : 128 * i + 128], pick)
        edge_send[pl.ds(pl.multiple_of(step * 128, 128), 128), :] = edge.astype(BF16)


class Place:
    def __init__(self):
        self.band = lax.axis_index("band")
        dom = lax.axis_index("domain")
        self.x, self.y = dom // 32, (dom // 8) % 4
        self.z, self.core = (dom // 2) % 4, dom % 2
        self.here = self.x * 4 + self.y
        self.zz = self.band * 4 + self.z
        self.partner = self.at(self.band, self.x, self.y, self.z, 1 - self.core)
        self.opposite = (1 - self.band, dom)
        self.next_x = (self.band, (dom + 8) % 128)
        self.last_x = (self.band, (dom + 120) % 128)
        self.next_y = (self.band, (dom // 8) * 8 + (dom + 1) % 8)
        self.last_y = (self.band, (dom // 8) * 8 + (dom + 7) % 8)

    @staticmethod
    def at(b, xx, yy, zl, cc):
        return (b, ((xx * 4 + yy) * 4 + zl) * 2 + cc)

    def xy_peer(self, k):
        xx, yy = (self.x + k // 4) % 4, (self.y + k % 4) % 4
        return self.at(self.band, xx, yy, self.z, self.core), xx * 4 + yy

    def xy_source(self, k):
        return ((self.x + 4 - k // 4) % 4) * 4 + (self.y + 4 - k % 4) % 4

    def z_peer(self, k):
        other = (self.zz + k) % 8
        return self.at(other // 4, self.x, self.y, other % 4, self.core)

    def greet(self, y_too):
        barrier = pltpu.get_barrier_semaphore()
        peers = [self.partner]
        peers += [self.xy_peer(k)[0] for k in range(1, 16)]
        peers += [self.z_peer(k) for k in range(1, 8)]
        if y_too:
            band, dom = self.next_y
            peers.append((band, jnp.where(self.core == 0, self.last_y[1], dom)))
        for peer in peers:
            pl.semaphore_signal(barrier, inc=1, device_id=peer, device_id_type=MESH)
        pl.semaphore_wait(barrier, len(peers))


def remote(src, dst, send, recv, device):
    return pltpu.make_async_remote_copy(
        src_ref=src, dst_ref=dst, send_sem=send, recv_sem=recv, device_id=device, device_id_type=MESH
    )


class Bulk:
    def __init__(self, pieces, device, sems, first, condition=None, other=None):
        self.sems, self.first, self.device = sems, first, device
        self.pieces, self.condition, self.other = pieces, condition, other
        self.started = 0

    def copy(self, i):
        src, dst = self.pieces[i]
        return remote(src, dst, self.sems[0].at[self.first + i], self.sems[1].at[self.first + i], self.device)

    def start(self, count=None):
        stop = len(self.pieces) if count is None else self.started + count

        def body():
            for i in range(self.started, stop):
                self.copy(i).start()

        if self.condition is None:
            body()
        else:
            pl.when(self.condition)(body)
        self.started = stop

    def wait(self):
        if self.condition is None:
            for i in range(len(self.pieces)):
                self.copy(i).wait()
            return

        @pl.when(self.condition)
        def _():
            for i in range(len(self.pieces)):
                self.copy(i).wait_send()

        @pl.when(self.other)
        def _():
            for i in range(len(self.pieces)):
                self.copy(i).wait_recv()


class Sum:
    scratch_count = 4 + 10

    def __init__(self, place, both, pay, out, scratch):
        self.place, self.both, self.pay, self.out = place, both, pay, out
        self.part = (out.shape[-2] if pay is None else pay.shape[1]) // 32
        self.half, self.whole, self.got, self.along = scratch[:4]
        self.s1, self.r1, self.s2, self.r2, self.s3, self.r3, self.s4, self.r4, self.s5, self.r5 = scratch[4:14]

    @staticmethod
    def scratch(n, height=256, wire=F32):
        dma = pltpu.SemaphoreType.DMA
        return [
            pltpu.VMEM((n, height // 2, 128), wire),
            pltpu.VMEM((n, height // 2, 128), wire),
            pltpu.VMEM((16, n, height // 32, 128), wire),
            pltpu.VMEM((8, n, height // 32, 128), wire),
            dma((1,)),
            dma((1,)),
            dma((16,)),
            dma((16,)),
            dma((8,)),
            dma((8,)),
            dma((16,)),
            dma((16,)),
            dma((16,)),
            dma((16,)),
        ]

    def rows(self, start, count=1):
        return pl.ds(pl.multiple_of(start * self.part, self.part), count * self.part)

    def first(self):
        p = self.place
        theirs = self.rows((1 - p.core) * 16, 16)
        return remote(self.pay.at[:, theirs, :], self.half, self.s1.at[0], self.r1.at[0], p.partner)

    def second(self, k):
        device, there = self.place.xy_peer(k)
        return remote(self.whole.at[:, self.rows(there), :], self.got.at[k], self.s2.at[k], self.r2.at[k], device)

    def third(self, k):
        p = self.place
        return remote(self.along.at[p.zz], self.along.at[p.zz], self.s3.at[k], self.r3.at[k], p.z_peer(k))

    def spot(self, row):
        rows = self.rows(self.place.core * 16 + row)
        return self.out.at[:, :, rows, :] if self.both else self.out.at[:, rows, :]

    def fourth(self, k, row):
        spot = self.spot(row)
        return remote(spot, spot, self.s4.at[k], self.r4.at[k], self.place.xy_peer(k)[0])

    def fifth(self, k, row):
        spot = self.spot(row)
        return remote(spot, spot, self.s5.at[k], self.r5.at[k], self.place.partner)

    def part1(self):
        self.first().start()

    def part2(self):
        self.first().wait()
        mine = self.rows(self.place.core * 16, 16)
        both = self.pay[:, mine, :].astype(F32) + self.half[...].astype(F32)
        self.whole[...] = both.astype(self.whole.dtype)
        for k in range(1, 16):
            self.second(k).start()

    def partial(self):
        for k in range(1, 16):
            self.second(k).wait()
        total = self.whole[:, self.rows(self.place.here), :]
        for k in range(1, 16):
            total = total + self.got[k]
        return total

    def part3(self, total=None):
        self.along[self.place.zz] = self.partial() if total is None else total
        for k in range(1, 8):
            self.third(k).start()

    def part4(self):
        p = self.place
        for k in range(1, 8):
            self.third(k).wait()
        along = [self.along[i].astype(F32) for i in range(8)]
        lower = along[0] + along[1] + along[2] + along[3]
        upper = along[4] + along[5] + along[6] + along[7]
        rows = self.rows(p.core * 16 + p.here)
        if self.both:
            self.out[0, :, rows, :] = lower
            self.out[1, :, rows, :] = upper
        else:
            self.out[:, rows, :] = lower + upper
        for k in range(1, 16):
            self.fourth(k, p.here).start()
        self.fifth(0, p.here).start()

    def part5(self):
        p = self.place
        for k in range(1, 16):
            source = p.xy_source(k)
            self.fourth(k, source).wait_recv()
            self.fifth(k, source).start()

    def end(self):
        p = self.place
        for k in range(1, 16):
            self.fourth(k, p.here).wait_send()
        for k in range(16):
            self.fifth(k, p.here).wait()


def invert_block(block):
    lane = lax.broadcasted_iota(jnp.int32, (8, 128), 1)
    sub = lax.broadcasted_iota(jnp.int32, (8, 128), 0)
    rows = [block[8 * p : 8 * p + 8] for p in range(16)]
    for p in range(16):
        k = 8 * p
        panel = rows[p]
        d = [[jnp.broadcast_to(panel[i : i + 1, k + j : k + j + 1], (8, 128)) for j in range(i + 1)] for i in range(8)]
        inside = (lane >= k) & (lane < k + 8)
        start = jnp.where(inside, (lane == k + sub).astype(F32), panel)
        acc = [jnp.broadcast_to(start[s : s + 1, :], (8, 128)) for s in range(8)]
        done = []
        for j in range(8):
            r = lax.rsqrt(d[j][j])
            xj = acc[j] * r
            done.append(xj)
            low = [None] * 8
            for i in range(j + 1, 8):
                low[i] = d[i][j] * r
            for i in range(j + 1, 8):
                for m in range(j + 1, i + 1):
                    d[i][m] = d[i][m] - low[i] * low[m]
                acc[i] = acc[i] - low[i] * xj
        x = done[0]
        for s in range(1, 8):
            x = jnp.where(sub == s, done[s], x)
        rows[p] = x
        if p < 15:
            ahead = jnp.where(inside, 0.0, rows[p + 1])
            pick = lane == k + 8 + sub
            for r in range(8):
                ahead = ahead - jnp.sum(jnp.where(pick, done[r], 0.0), axis=1, keepdims=True) * done[r]
            rows[p + 1] = ahead
        if p < 14:
            right = jnp.where(lane >= k + 16, x, 0.0)
            update = fdot(right, x, TN)
            for q in range(p + 2, 16):
                rows[q] = jnp.where(inside, 0.0, rows[q]) - update[8 * q : 8 * q + 8]
    whole = jnp.concatenate(rows, axis=0)
    rr = lax.broadcasted_iota(jnp.int32, (128, 128), 0)
    cc = lax.broadcasted_iota(jnp.int32, (128, 128), 1)
    return jnp.where(cc <= rr, whole, 0.0)


def eliminate_step(c, offset, j, between=None):
    blocks = c.shape[0] // 128
    rr = lax.broadcasted_iota(jnp.int32, (128, 128), 0)
    cc = lax.broadcasted_iota(jnp.int32, (128, 128), 1)
    rows, cols = slice(128 * j, 128 * j + 128), slice(offset + 128 * j, offset + 128 * j + 128)
    inverse = invert_block(c[rows, cols])
    c[rows, cols] = (rr == cc).astype(F32)
    c[rows, :] = fdot(inverse, c[rows, :])
    if between is not None:
        between()
    for i in range(j + 1, blocks):
        below = slice(128 * i, 128 * i + 128)
        across = slice(offset + 128 * i, offset + 128 * i + 128)
        factor = c[rows, across]
        c[below, cols] = jnp.zeros((128, 128), F32)
        c[below, :] = c[below, :] - fdot(factor, c[rows, :], TN)


def clear_right(c, offset):
    for i in range(c.shape[0] // 128):
        for j in range(i + 1, c.shape[0] // 128):
            c[128 * i : 128 * i + 128, offset + 128 * j : offset + 128 * j + 128] = jnp.zeros((128, 128), F32)


def spread(c, slabs, tiles, offset):
    for t, (r, col) in enumerate(tiles):
        for h in range(2):
            lo = offset + 256 * col + 128 * h
            c[256 * r : 256 * r + 256, lo : lo + 128] = slabs(2 * t + h)


def first_factor_kernel(
    orb, orb_far, pot, s_sum, w, h_part, half, edge, keep, recv, edge_recv, *scratch
):
    place = Place()
    s_pay, h_pay = scratch[23:25]
    own = Sum(place, True, h_pay, None, scratch[25:39])
    total = Sum(place, True, s_pay, s_sum, scratch[:14])
    sems = scratch[14:16]
    xlo, xhi, ylo, yhi, hpsi, send, edge_send = scratch[16:23]
    rows = lambda i: pl.ds(32 * i, 32)
    pieces = [(edge_send, edge_recv)] + [(send.at[rows(i), :], recv.at[rows(i), :]) for i in range(16)]
    swap = Bulk(pieces, place.opposite, sems, 0)
    quarters = [pl.ds(128 * i, 128) for i in range(4)]
    x_up = Bulk(
        [(orb_far.at[q, pl.ds(1024, 1024)], xlo.at[q, :]) for q in quarters], place.next_x, sems, 17
    )
    x_down = Bulk([(orb_far.at[q, pl.ds(0, 1024)], xhi.at[q, :]) for q in quarters], place.last_x, sems, 21)
    y_up = Bulk(
        [(orb_far.at[:, pl.ds(512 * a + 256, 256)], ylo.at[:, pl.ds(256 * a, 256)]) for a in range(4)],
        place.next_y,
        sems,
        25,
    )
    y_down = Bulk(
        [(orb_far.at[:, pl.ds(512 * a, 256)], yhi.at[:, pl.ds(256 * a, 256)]) for a in range(4)],
        place.last_y,
        sems,
        29,
    )
    place.greet(True)
    y_up.start()
    pack(place.band, orb, pot, s_pay, send, keep, edge_send)
    total.part1()
    total.part2()
    x_up.start()
    x_down.start()
    total.part3()
    y_down.start()
    edge_differences(place.band, orb, edge)
    total.part4()
    swap.start(6)
    total.part5()
    swap.start(3)
    x_up.wait()
    x_down.wait()
    y_up.wait()
    y_down.wait()
    swap.start(3)
    hamiltonian(place.band, orb, xlo, xhi, ylo, yhi, pot, hpsi, half)
    swap.start()
    for t, (r, c) in enumerate(TILES_LOW):
        tile = bdot(hpsi[256 * r : 256 * r + 256, :], orb[256 * c : 256 * c + 256, :], NT)
        store_tall(h_pay, t, tile)
    own.part1()
    total.end()
    w[256:512, 0:256] = jnp.zeros((256, 256), F32)
    spread(w, lambda i: s_sum[0, i], TILES_UP, 0)
    eliminate_step(w, 0, 0)
    own.part2()
    for j in range(1, 4):
        eliminate_step(w, 0, j)
    clear_right(w, 0)
    h_part[...] = own.partial()
    swap.wait()


def second_factor_kernel(
    s, h_part, half, edge, keep, keep_far, recv, edge_recv, w0, c, own_sum, cross_sum, rest, *scratch
):
    place = Place()
    x_pay, x_sum, cross_pay, cross_s = scratch[42:46]
    over = Sum(place, False, x_pay, x_sum, scratch[:14])
    own = Sum(place, True, None, own_sum, scratch[14:28])
    cross = Sum(place, False, cross_pay, cross_sum, scratch[28:42])
    sems = scratch[46:48]
    rows = lambda i: pl.ds(32 * i, 32)
    pieces = [(keep_far.at[rows(i), :], rest.at[rows(i), :]) for i in range(16)]
    tail = Bulk(pieces, place.opposite, sems, 0, place.band == 0, place.band == 1)
    place.greet(False)
    own.part3(h_part[...])
    tail.start(3)
    cross_products(place.band, keep, recv, x_pay)
    over.part1()
    cross_products(place.band, half, recv, cross_pay, edge, edge_recv)
    over.part2()
    cross.part1()
    over.part3()
    tail.start(1)
    over.part4()
    tail.start(2)
    cross.part2()
    own.part4()
    over.part5()
    tail.start(2)
    over.end()
    for t, (r, col) in enumerate(TILES_ALL):
        for h in range(2):
            lo = 256 * col + 128 * h
            cross_s[256 * r : 256 * r + 256, lo : lo + 128] = x_sum[2 * t + h]
    first = split(w0[...])
    low = split(dot3(split(cross_s[...]), first, NT))
    c[256:512, 512:768] = jnp.zeros((256, 256), F32)
    spread(c, lambda i: s[1, i], TILES_UP, 512)
    c[:, 512:1024] = c[:, 512:1024] - dot3(low, low, NT)
    c[:, 0:512] = -dot3(low, first)
    cross.part3()
    tail.start(1)
    own.part5()
    more = lambda: tail.start(1)
    eliminate_step(c, 512, 0, more)
    more()
    cross.part4()
    eliminate_step(c, 512, 1, more)
    more()
    eliminate_step(c, 512, 2, more)
    tail.start()
    cross.part5()
    eliminate_step(c, 512, 3)
    clear_right(c, 512)
    own.end()
    cross.end()
    tail.wait()


def split(a):
    high = a.astype(BF16)
    return high, (a - high.astype(F32)).astype(BF16)


def dot3(a, b, dims=NN):
    return bdot(a[0], b[0], dims) + (bdot(a[0], b[1], dims) + bdot(a[1], b[0], dims))


def last_kernel(
    s, hown, cross, w0, c, recv_far, rest_far, own_far, h_sub, rotated, rot_other, rot_own, wh, wl, mh, ml, g, *scratch
):
    band = lax.axis_index("band")
    recv, rest, own, out, sems = scratch
    loads = [
        pltpu.make_async_copy(far, near, sems.at[i])
        for i, (far, near) in enumerate(((recv_far, recv), (rest_far, rest), (own_far, own)))
    ]
    for load in loads:
        load.start()

    @pl.when(band == 0)
    def _():
        rot_own[...] = w0[...].astype(BF16)
        rot_other[...] = jnp.zeros((512, 512), BF16)

    @pl.when(band == 1)
    def _():
        rot_own[...] = c[:, 512:1024].astype(BF16)
        rot_other[...] = c[:, 0:512].astype(BF16)

    for load in loads:
        load.wait()
    rotate(band, rot_other, rot_own, recv, rest, own, out)
    store = pltpu.make_async_copy(out, rotated, sems.at[3])
    store.start()

    for r in range(4):
        source = w0 if r < 2 else c
        base = 256 * (r % 2)
        width = 512 if r < 2 else 1024
        high, lowpart = split(source[base : base + 256, :])
        wh[256 * r : 256 * r + 256, 0:width] = high
        wl[256 * r : 256 * r + 256, 0:width] = lowpart

    rr = lax.broadcasted_iota(jnp.int32, (256, 256), 0)
    cc = lax.broadcasted_iota(jnp.int32, (256, 256), 1)
    weight = jnp.where(cc < rr, 1.0, jnp.where(cc == rr, 0.5, 0.0)).astype(F32)

    def wide(tall):
        return jnp.concatenate([tall[0:256, :], tall[256:512, :]], axis=1)

    half = {}
    for b in range(2):
        for t, (r, col) in enumerate(TILES_LOW):
            tile = wide(hown[b, t])
            if r == col:
                tile = tile * weight
            half[2 * b + r, 2 * b + col] = split(tile)
    for t, (r, col) in enumerate(TILES_ALL):
        half[2 + r, col] = split(wide(cross[t]))

    def stripe(high, lowpart, k):
        rows, cols = slice(256 * k, 1024), slice(256 * k, 256 * k + 256)
        return high[rows, cols], lowpart[rows, cols]

    def square(high, lowpart, r, col):
        rows, cols = slice(256 * r, 256 * r + 256), slice(256 * col, 256 * col + 256)
        return high[rows, cols], lowpart[rows, cols]

    for col in range(4):
        g[256 * col : 1024, :] = dot3(stripe(wh, wl, col), half[col, col])
        for k in range(col + 1, 4):
            g[256 * k : 1024, :] = g[256 * k : 1024, :] + dot3(stripe(wh, wl, k), half[k, col])
        high, lowpart = split(g[256 * col : 1024, :])
        mh[256 * col : 1024, 256 * col : 256 * col + 256] = high
        ml[256 * col : 1024, 256 * col : 256 * col + 256] = lowpart

    vmean = jnp.sum(s[0, 0, 128:136, :]) / (128 * CELLS)
    shift = jnp.where(rr == cc, vmean, 0.0)

    for col in range(4):
        cols = slice(256 * col, 256 * col + 256)
        h_sub[:, cols] = dot3(stripe(mh, ml, 0), square(wh, wl, col, 0), NT)
        for k in range(1, col + 1):
            rows = slice(256 * k, 1024)
            h_sub[rows, cols] = h_sub[rows, cols] + dot3(stripe(mh, ml, k), square(wh, wl, col, k), NT)
    for r in range(4):
        up = slice(256 * r, 256 * r + 256)
        for col in range(r + 1):
            across = slice(256 * col, 256 * col + 256)
            if r == col:
                tile = h_sub[up, up]
                h_sub[up, up] = tile + tile.T - shift
            else:
                tile = h_sub[up, across] + h_sub[across, up].T
                h_sub[up, across] = tile
                h_sub[across, up] = tile.T
    store.wait()


def circle_weights():
    row = lax.broadcasted_iota(jnp.int32, (128, 128), 0)
    col = lax.broadcasted_iota(jnp.int32, (128, 128), 1)
    return row, col, step_weights((row - col + 128) % 128)


def step_weights(away):
    near = (away == 1) | (away == 127)
    far = (away == 2) | (away == 126)
    return jnp.where(near, 16.0, jnp.where(far, -1.0, 0.0))


def edge_differences(band, orb, edge):
    row, _, _ = circle_weights()
    _, owner, level = edge_cells()
    weights = jnp.where(row < 64, step_weights((row - level + 128) % 128), 0.0)

    @pl.loop(0, 4)
    def _(step):
        rows = pl.ds(pl.multiple_of(step * 128, 128), 128)
        total = jnp.zeros((128, 128), F32)
        for i in range(16):
            total = total + bdot(orb[rows, 128 * i : 128 * i + 128], jnp.where(owner == i, weights, 0.0).astype(BF16))
        edge[rows, :] = jnp.where(band == 1, total * (-0.5 / 12.0), 0.0).astype(BF16)


def hamiltonian(band, orb, xlo, xhi, ylo, yhi, pot, hpsi, half):
    row, col, weights = circle_weights()
    full = jnp.where(row == col, -90.0, weights)
    outer = jnp.where((band == 0) & (row < 64) & (col >= 64), weights, 0.0)
    circles = jnp.concatenate([full, outer], axis=1).astype(BF16)
    pack = jnp.concatenate(packers(64 - 64 * band), axis=0)
    n = 32

    @pl.loop(0, HALF // n, unroll=2)
    def _(step):
        rows = pl.ds(pl.multiple_of(step * n, n), n)

        def slab(ref, i):
            return ref[rows, 128 * i : 128 * i + 128]

        def cell(a, b):
            if a < 0:
                return slab(xlo, (a + 2) * 4 + b)
            if a > 3:
                return slab(xhi, (a - 4) * 4 + b)
            if b < 0:
                return slab(ylo, a * 2 + b + 2)
            if b > 3:
                return slab(yhi, a * 2 + b - 4)
            return slab(orb, a * 4 + b)

        cells = jnp.concatenate([cell(i // 4, i % 4) for i in range(16)], axis=0)
        along = bdot(cells, circles)
        parts = [[], []]
        for i in range(16):
            a, b = i // 4, i % 4
            field = lambda i, j: cell(i, j).astype(F32)
            near = (field(a - 1, b) + field(a + 1, b)) + (field(a, b - 1) + field(a, b + 1))
            far = (field(a - 2, b) + field(a + 2, b)) + (field(a, b - 2) + field(a, b + 2))
            here = slice(n * i, n * i + n)
            value = (16.0 * near - far + along[here, :128]) * (-0.5 / 12.0) + pot[i : i + 1, :] * field(a, b)
            hpsi[rows, 128 * i : 128 * i + 128] = value.astype(BF16)
            parts[i % 2].append((value + along[here, 128:] * (0.5 / 12.0)).astype(BF16))
        sides = [jnp.concatenate(part, axis=0) for part in parts]
        packed = bdot(jnp.concatenate(sides, axis=1), pack)
        for m in range(8):
            half[rows, 128 * m : 128 * m + 128] = packed[n * m : n * m + n].astype(BF16)


def store_tall(out, t, tile):
    out[t, 0:256, :] = tile[:, :128].astype(out.dtype)
    out[t, 256:512, :] = tile[:, 128:].astype(out.dtype)


def cross_products(band, half, recv, out, edge=None, edge_recv=None):
    def products(left, right, corner):
        for t, (r, c) in enumerate(TILES_ALL):
            up, across = slice(256 * r, 256 * r + 256), slice(256 * c, 256 * c + 256)
            tile = bdot(left[up, 0:1024], right[across, 0:1024], NT)
            if corner:
                lane = lax.broadcasted_iota(jnp.int32, (256, 128), 1)
                corner_part = jnp.where(lane // 64 == c, edge[up, :].astype(F32), 0.0).astype(BF16)
                tile = tile + bdot(corner_part, edge_recv[...], NT)
            if edge is None:
                out[2 * t] = tile[:, :128]
                out[2 * t + 1] = tile[:, 128:]
            else:
                store_tall(out, t, tile)

    @pl.when(band == 1)
    def _():
        products(half, recv, edge is not None)

    @pl.when(band == 0)
    def _():
        products(recv, half, False)


def rotate(band, rot_other, rot_own, recv, rest, own, out):
    @pl.when(band == 0)
    def _():
        for i in range(4):
            there = slice(512 * i, 512 * i + 512)
            out[:, there] = bdot(rot_own[...], own[:, there]).astype(BF16)

    @pl.when(band == 1)
    def _():
        low = jnp.concatenate(packers(0), axis=0)
        high = jnp.concatenate(packers(64), axis=0)
        unpack = jnp.concatenate([low, high], axis=1)
        for m in range(8):
            cols = slice(128 * m, 128 * m + 128)
            other = bdot(jnp.concatenate([recv[:, cols], rest[:, cols]], axis=1), unpack, NT).astype(BF16)
            there = slice(256 * m, 256 * m + 256)
            total = bdot(rot_own[...], own[:, there]) + bdot(rot_other[...], other)
            out[:, there] = total.astype(BF16)


def shards(orbitals, potential):
    orb = orbitals.reshape(HALF, CELLS)
    pot = potential.reshape(16, 128)
    slab = lambda n: jax.ShapeDtypeStruct((n, 256, 128), F32)
    square = lambda n, t: jax.ShapeDtypeStruct((n, n), t)
    wide = lambda n: jax.ShapeDtypeStruct((HALF, n), BF16)
    tall = lambda n, t, *lead: jax.ShapeDtypeStruct(lead + (n, 512, 128), t)
    two = lambda n: jax.ShapeDtypeStruct((2, n, 256, 128), F32)
    dma = pltpu.SemaphoreType.DMA
    part = jax.ShapeDtypeStruct((3, 16, 128), F32)
    corner = jax.ShapeDtypeStruct((256, 128), BF16)
    s_sum, w0, h_part, half, edge, keep, recv, edge_recv = call(
        first_factor_kernel,
        [two(6), square(512, F32), part, wide(1024), wide(128), wide(1024), wide(1024), corner],
        (orb, orb, pot),
        "first_factor",
        scratch=Sum.scratch(6)
        + [dma((33,)), dma((33,))]
        + [pltpu.VMEM((HALF, n), BF16) for n in (1024, 1024, 1024, 1024, CELLS, 1024)]
        + [pltpu.VMEM((256, 128), BF16), pltpu.VMEM((6, 256, 128), F32), pltpu.VMEM((3, 512, 128), F32)]
        + Sum.scratch(3, 512),
        collective=0,
        far_in=(1,),
        far_out=(6, 7),
    )
    c, h_sum, hx_sum, rest = call(
        second_factor_kernel,
        [jax.ShapeDtypeStruct((HALF, 1024), F32), tall(3, F32, 2), tall(4, F32), wide(1024)],
        (s_sum, h_part, half, edge, keep, keep, recv, edge_recv, w0),
        "second_factor",
        scratch=Sum.scratch(8)
        + Sum.scratch(3, 512)
        + Sum.scratch(4, 512)
        + [pltpu.VMEM((8, 256, 128), F32)] * 2
        + [pltpu.VMEM((4, 512, 128), F32), pltpu.VMEM((512, 512), F32)]
        + [dma((16,)), dma((16,))],
        collective=1,
        far_in=(5,),
        far_out=(3,),
    )
    h_sub, rotated = call(
        last_kernel,
        [square(1024, F32), wide(CELLS)],
        (s_sum, h_sum, hx_sum, w0, c, recv, rest, orb),
        "subspace_matrix",
        scratch=[pltpu.VMEM((HALF, HALF), BF16)] * 2
        + [pltpu.VMEM((1024, 1024), BF16)] * 4
        + [pltpu.VMEM((1024, 256), F32)]
        + [pltpu.VMEM((HALF, n), BF16) for n in (1024, 1024, CELLS, CELLS)]
        + [dma((4,))],
        far_in=(5, 6, 7),
        far_out=(1,),
    )
    return rotated.reshape(orbitals.shape), h_sub


def solution(mesh):
    in_specs = (P("band", "domain", None), P("domain", None))
    out_specs = (P("band", "domain", None), P())
    return jax.shard_map(shards, mesh=mesh, in_specs=in_specs, out_specs=out_specs, check_vma=False)
```
